128 devices in a mesh: seq: 32 (over y, x_hi, z), tp: 4 (over x_lo, core).
Axes of the slice: x: 4 (x_hi: 2, x_lo: 2; x = x_hi * 2 + x_lo), y: 4, z: 4, core: 2. Of those that a mesh axis runs over, the one named last changes fastest.
Arguments:
- gate_pre: bfloat16 [4096, 7168], P('seq', 'tp'), may hold values from -6 to 6
- up_pre: bfloat16 [4096, 7168], P('seq', 'tp'), may hold values from -6 to 6
- token_weight: bfloat16 [4096], P('seq'), may hold values from 0.099609375 to 1
- query_grad: float32 [7168, 4096], P('tp', 'seq'), may hold values from -6 to 6
Outputs:
- solution: float32 [7168, 4096], P('tp', 'seq')
- residual: float32 [7168, 4096], P('tp', 'seq')
The draws below stay inside these ranges and needn't reach their ends.
All inputs are finite; a program needn't handle non-finite values.
Results may differ from the reference program's by a relative error of at most 0.0082.
Values may be sent and summed in bfloat16 or wider, within the bound.
A program may use at most 64 MiB of HBM per device.

```python
import math
import jax
import jax.numpy as jnp

D = 4096
FFW = 7168
ITERS = 2
TOKENS = 4096
N_SEQ = 32
N_TP = 4


def block_levels(key):
    key = jax.random.fold_in(key, 11)
    order = jax.random.permutation(key, N_TP).astype(jnp.float32)
    jitter = jax.random.uniform(jax.random.fold_in(key, 1), (N_TP,), jnp.float32)
    return jnp.exp(-1.0 + 1.8 * (order + jitter) / N_TP)


def draw_gate_pre(key, part):
    levels = block_levels(key)
    key = jax.random.fold_in(key, 3)
    base = jax.random.normal(key, (TOKENS, FFW), jnp.float32)
    factor = jnp.repeat(levels, FFW // N_TP)
    return jnp.clip(base * factor[None, :], -6.0, 6.0).astype(jnp.bfloat16)


def draw_up_pre(key, part):
    levels = block_levels(key)
    key = jax.random.fold_in(key, 5)
    base = jax.random.normal(key, (TOKENS, FFW), jnp.float32)
    factor = jnp.repeat(levels, FFW // N_TP)
    return jnp.clip(base * factor[None, :], -6.0, 6.0).astype(jnp.bfloat16)


def draw_query_grad(key, part):
    key = jax.random.fold_in(key, 7)
    loudness = jnp.exp(jax.random.uniform(jax.random.fold_in(key, 1), (N_TP, N_SEQ), jnp.float32, -1.5, 1.5))
    base = jax.random.normal(key, (FFW, D), jnp.float32)
    factor = jnp.repeat(jnp.repeat(loudness, FFW // N_TP, axis=0), D // N_SEQ, axis=1)
    return jnp.clip(base * factor, -6.0, 6.0)


def block_scale(rng, extent, split, low, high):
    def one(dim, parts):
        draws = jax.random.uniform(jax.random.fold_in(jax.random.fold_in(rng, 6), dim), (parts,), jnp.float32, low / len(split), high / len(split))
        return jnp.repeat(jnp.exp(draws), extent[dim] // parts).reshape((-1,) + (1,) * (len(extent) - dim - 1))

    level = one(*split[0])
    for cut in split[1:]:
        level = level * one(*cut)
    return level


def setup_inputs(seed: int = 0) -> dict:
    seeds = jax.random.split(jax.random.key(seed), 5)
    return {
        "gate_pre": draw_gate_pre(jax.random.fold_in(seeds[4], 71), 0),
        "up_pre": draw_up_pre(jax.random.fold_in(seeds[4], 71), 0),
        "token_weight": jnp.clip(jnp.exp(math.log(1.0) - 2.306499 * jax.random.uniform(seeds[2], (TOKENS,), jnp.float32) ** block_scale(seeds[2], (TOKENS,), ((0, 32),), -0.2, 0.2)), 0.099609375, 1.0).astype(jnp.bfloat16),
        "query_grad": draw_query_grad(jax.random.fold_in(seeds[4], 71), 0),
    }


DAMP = 1.0


def reference(gate_pre, up_pre, token_weight, query_grad):
    hidden = (jax.nn.silu(gate_pre.astype(jnp.float32)) * up_pre.astype(jnp.float32)).astype(jnp.bfloat16)
    weight = token_weight.astype(jnp.float32)[:, None] / hidden.shape[0]

    def apply(direction):
        image = jnp.dot(hidden, direction.astype(jnp.bfloat16), preferred_element_type=jnp.float32)
        scaled = (image * weight).astype(jnp.bfloat16)
        return jnp.dot(hidden.T, scaled, preferred_element_type=jnp.float32) + DAMP * direction

    solution = jnp.zeros_like(query_grad)
    residual = query_grad
    direction = query_grad
    norm_now = jnp.sum(residual * residual)
    for step in range(ITERS):
        image = apply(direction)
        alpha = norm_now / jnp.sum(direction * image)
        solution = solution + alpha * direction
        residual = residual - alpha * image
        if step + 1 < ITERS:
            norm_next = jnp.sum(residual * residual)
            direction = residual + (norm_next / norm_now) * direction
            norm_now = norm_next
    return solution, residual
```

```python
import jax
import jax.numpy as jnp
from jax import lax
from jax.experimental import pallas as pl
from jax.experimental.pallas import tpu as pltpu
from jax.sharding import PartitionSpec as P

DAMP = 1.0
F32, BF16 = jnp.float32, jnp.bfloat16
MESH = pl.DeviceIdType.MESH

B = 128
FQ = 1792
R = 32
UNITS = [(0, 0), (1, 0), (3, 0), (2, 0), (0, 1), (0, 3), (0, 2), (1, 1), (1, 3), (3, 1), (3, 3), (2, 1), (1, 2), (2, 3), (3, 2), (2, 2)]
SLOT = {u: i for i, u in enumerate(UNITS)}
UT = 2 * B
T = len(UNITS) * UT
GROUPS0 = [(0, 4), (4, 7), (7, 11), (11, 13), (13, 15), (15, 16)]
GROUPS1 = [(0, 2), (2, 4), (4, 6), (6, 8), (8, 10), (10, 12), (12, 14), (14, 16)]
NSEM = 192


def kernel(gate, up, tw, q, x_out, r_out, H, nblk, hl_s, hl, qv, qb, z0, zb, z1, yown, yst, rs, sT, wb, wrow, acc, sc, fin_s, fin, ssem, rsem):
    s, t = lax.axis_index("seq"), lax.axis_index("tp")
    y, xh, z = s // 8, (s // 4) % 2, s % 4
    xl, k = t // 2, t % 2
    x = xh * 2 + xl

    def dev(x, y, z, k):
        return (y * 8 + (x // 2) * 4 + z, (x % 2) * 2 + k)

    def ystep(d):
        return dev(x, (y + d) % 4, z, k)

    def zstep(d):
        return dev(x, y, (z + d) % 4, k)

    def xstep(d):
        return dev((x + d) % 4, y, z, k)

    sib = dev(x, y, z, 1 - k)
    partner = dev((x + 2) % 4, y, z, 1 - k)
    moved = k != xh

    barrier = pltpu.get_barrier_semaphore()
    peers = [sib, partner]
    for step in (xstep, ystep, zstep):
        peers += [step(1), step(2), step(3)]
    for p in peers:
        pl.semaphore_signal(barrier, inc=1, device_id=p, device_id_type=MESH)
    pl.semaphore_wait(barrier, len(peers))

    count = [0]
    sent, sent_moved = [], []

    def remote(src, dst, device, log=True):
        i = count[0]
        count[0] += 1
        cp = pltpu.make_async_remote_copy(src_ref=src, dst_ref=dst, send_sem=ssem.at[i], recv_sem=rsem.at[i], device_id=device, device_id_type=MESH)
        (sent if log else sent_moved).append(cp)
        return cp

    def push(src, dst, device):
        cp = remote(src, dst, device)
        cp.start()
        return cp

    @pl.loop(0, B // 16)
    def _(i):
        rows = pl.ds(pl.multiple_of(i * 16, 16), 16)
        g, u = gate[rows, :].astype(F32), up[rows, :].astype(F32)
        nblk[rows, :] = (g / (1.0 + jnp.exp(-g)) * u).astype(BF16)

    wb[0, 16] = jnp.broadcast_to(tw[...].astype(F32) * (1.0 / T), (8, B))

    def block(yr, zr, core=0, off=0, n=B):
        return H.at[pl.ds(SLOT[yr, zr] * UT + core * B + off, n)]

    move_h = remote(nblk, block(0, 0), partner, log=False)
    move_w = remote(wb.at[0, 16], wb.at[0, 0], partner, log=False)
    move_q = remote(hl_s, hl, partner, log=False)

    @pl.when(moved)
    def _():
        move_h.start()
        move_w.start()

    @pl.when(jnp.logical_not(moved))
    def _():
        block(0, 0)[...] = nblk[...]
        wb[0, 0] = wb[0, 16]

    for i in range(FQ // B):
        cols = slice(i * B, (i + 1) * B)
        qt = q[cols, :].T
        hi = qt.astype(BF16)
        hl_s[:B, cols] = hi
        hl_s[B:, cols] = (qt - hi.astype(F32)).astype(BF16)

    @pl.when(moved)
    def _():
        move_q.start()
        move_h.wait_recv()

    def hop(yr, zr, axis, d, off, n):
        if axis == "y":
            return push(block(yr, zr, 0, off, n), block((yr - d) % 4, zr, 0, off, n), ystep(d))
        return push(block(yr, zr, 0, off, n), block(yr, (zr - d) % 4, 0, off, n), zstep(d))

    s1 = {(a, d): hop(0, 0, a, d, 0, B) for a in "yz" for d in (1, -1)}
    relays = {}

    def relay(yr, zr):
        relays[yr, zr] = push(block(yr, zr, 0), block(yr, zr, 1), sib)

    relay(0, 0)

    @pl.when(moved)
    def _():
        move_w.wait_recv()

    wy = [push(wb.at[0, 0], wb.at[0, (4 - d) % 4], ystep(d)) for d in (1, 2, 3)]

    s1["y", 1].wait_recv()
    s2 = [hop(3, 0, "y", 1, 0, 64)]
    s3 = {}
    s3["z", 3, 1], s3["z", 3, -1] = hop(3, 0, "z", 1, 0, 64), hop(3, 0, "z", -1, 0, 64)
    s1["y", -1].wait_recv()
    s2 += [hop(1, 0, "y", -1, 64, 64)]
    s3["z", 1, 1], s3["z", 1, -1] = hop(1, 0, "z", 1, 0, 64), hop(1, 0, "z", -1, 0, 64)
    s1["z", 1].wait_recv()
    s2 += [hop(0, 3, "z", 1, 0, 64)]
    s3["y", 3, 1], s3["y", 3, -1] = hop(0, 3, "y", 1, 64, 64), hop(0, 3, "y", -1, 64, 64)
    s1["z", -1].wait_recv()
    s2 += [hop(0, 1, "z", -1, 64, 64)]
    s3["y", 1, 1], s3["y", 1, -1] = hop(0, 1, "y", 1, 64, 64), hop(0, 1, "y", -1, 64, 64)
    for u in ((1, 0), (3, 0), (0, 1), (0, 3)):
        relay(*u)

    for cp in wy:
        cp.wait_recv()
    wz = [push(wb.at[0, pl.ds(0, 4)], wb.at[0, pl.ds(4 * ((4 - d) % 4), 4)], zstep(d)) for d in (1, 2, 3)]

    @pl.when(moved)
    def _():
        move_q.wait_recv()

    @pl.when(jnp.logical_not(moved))
    def _():
        hl[...] = hl_s[...]

    for j in range(4):
        base = ((x + j) % 4) * R
        hi = hl[pl.ds(pl.multiple_of(base, R), R), :]
        lo = hl[pl.ds(pl.multiple_of(base + B, R), R), :]
        qb[j * R : (j + 1) * R, :] = hi
        qv[j * R : (j + 1) * R, :] = hi.astype(F32) + lo.astype(F32)
    z0[...] = jnp.zeros_like(z0)
    z1[...] = jnp.zeros_like(z1)
    acc[...] = jnp.zeros_like(acc)

    for cp in s2:
        cp.wait_recv()
    s3["z", 2, 1], s3["z", 2, -1] = hop(2, 0, "z", 1, 0, 64), hop(2, 0, "z", -1, 0, 64)
    s3["y", 2, 1], s3["y", 2, -1] = hop(0, 2, "y", 1, 64, 64), hop(0, 2, "y", -1, 64, 64)
    relay(2, 0)
    relay(0, 2)
    for cp in wz:
        cp.wait_recv()
    ws = push(wb.at[0, pl.ds(0, 16)], wb.at[1, pl.ds(0, 16)], sib)

    def cols_of(group):
        return group[0] * UT, (group[1] - group[0]) * UT

    def image(it, p, group):
        @pl.loop(group[0], group[1])
        def _(u):
            at = pl.ds(pl.multiple_of(u * UT, UT), UT)
            part = lax.dot_general(p[...], H[at, :], (((1,), (1,)), ((), ())), preferred_element_type=F32)
            yown[it, :, at] = part[:R]
            yst[it, :, at] = part[R:].astype(BF16)

        c, n = cols_of(group)
        out = []
        for j in (2, 1, 3):
            out.append(push(yst.at[it, pl.ds((j - 1) * R, R), pl.ds(c, n)], rs.at[it, 3 - j, :, pl.ds(c, n)], xstep(j)))
        return out

    def reduce(it, group, copies):
        for cp in copies:
            cp.wait_recv()

        @pl.loop(group[0], group[1])
        def _(u):
            at = pl.ds(pl.multiple_of(u * UT, UT), UT)
            total = yown[it, :, at] + rs[it, 0, :, at].astype(F32) + rs[it, 1, :, at].astype(F32) + rs[it, 2, :, at].astype(F32)
            scaled = (total * wrow[0:1, at]).astype(BF16)
            sT[it, pl.ds(0, R), at] = scaled
            if it:
                acc[...] += total * scaled.astype(F32)

        c, n = cols_of(group)
        out = []
        for j in (2, 1, 3):
            out.append(push(sT.at[it, pl.ds(0, R), pl.ds(c, n)], sT.at[it, pl.ds((4 - j) * R, R), pl.ds(c, n)], xstep(j)))
        return out

    def back(it, zz, group, copies):
        for cp in copies:
            cp.wait_recv()

        @pl.loop(group[0], group[1])
        def _(u):
            at = pl.ds(pl.multiple_of(u * UT, UT), UT)
            zz[...] += jnp.dot(sT[it, :, at], H[at, :], preferred_element_type=F32)

    def wait_relays(group):
        for u in range(*group):
            relays[UNITS[u]].wait_recv()

    G = GROUPS0
    wait_relays(G[0])
    a0 = image(0, qb, G[0])
    wait_relays(G[1])
    a1 = image(0, qb, G[1])
    ws.wait_recv()
    for u, (yr, zr) in enumerate(UNITS):
        for c in range(2):
            wrow[0:8, u * UT + c * B : u * UT + (c + 1) * B] = wb[c, zr * 4 + yr]

    s4 = {}

    def onward(yr, zr, axis, d):
        off = {("z", 1): 0, ("z", -1): 32, ("y", 1): 64, ("y", -1): 96}[axis, d]
        return hop(yr, zr, axis, d, off, 32)

    s3["z", 3, 1].wait_recv()
    s4["z", 3, 1] = onward(3, 3, "z", 1)
    s3["z", 3, -1].wait_recv()
    s4["z", 3, -1] = onward(3, 1, "z", -1)
    s3["z", 1, 1].wait_recv()
    s4["z", 1, 1] = onward(1, 3, "z", 1)
    s3["z", 1, -1].wait_recv()
    s4["z", 1, -1] = onward(1, 1, "z", -1)
    s3["y", 3, 1].wait_recv()
    s4["y", 3, 1] = onward(3, 3, "y", 1)
    s3["y", 3, -1].wait_recv()
    s4["y", 3, -1] = onward(1, 3, "y", -1)
    s3["y", 1, 1].wait_recv()
    s4["y", 1, 1] = onward(3, 1, "y", 1)
    s3["y", 1, -1].wait_recv()
    s4["y", 1, -1] = onward(1, 1, "y", -1)
    for u in ((1, 1), (1, 3), (3, 1), (3, 3)):
        relay(*u)
    b0 = reduce(0, G[0], a0)
    b1 = reduce(0, G[1], a1)
    s3["z", 2, 1].wait_recv()
    s4["z", 2, 1] = onward(2, 3, "z", 1)
    s3["z", 2, -1].wait_recv()
    s4["z", 2, -1] = onward(2, 1, "z", -1)
    s3["y", 2, 1].wait_recv()
    s4["y", 2, 1] = onward(3, 2, "y", 1)
    s3["y", 2, -1].wait_recv()
    s4["y", 2, -1] = onward(1, 2, "y", -1)
    wait_relays(G[2])
    a2 = image(0, qb, G[2])
    back(0, z0, G[0], b0)
    back(0, z0, G[1], b1)

    def far(axis, i):
        for d in (1, -1):
            s4[axis, i, d].wait_recv()

    far("y", 1)
    relay(2, 1)
    far("z", 1)
    relay(1, 2)
    b2 = reduce(0, G[2], a2)
    wait_relays(G[3])
    a3 = image(0, qb, G[3])
    far("y", 3)
    relay(2, 3)
    far("z", 3)
    relay(3, 2)
    back(0, z0, G[2], b2)
    b3 = reduce(0, G[3], a3)
    wait_relays(G[4])
    a4 = image(0, qb, G[4])
    far("y", 2)
    far("z", 2)
    relay(2, 2)
    wait_relays(G[5])
    a5 = image(0, qb, G[5])
    b4 = reduce(0, G[4], a4)
    back(0, z0, G[3], b3)
    b5 = reduce(0, G[5], a5)
    back(0, z0, G[4], b4)
    back(0, z0, G[5], b5)

    zb[...] = z0[...].astype(BF16)

    def total_of(v):
        return jnp.sum(jnp.sum(v, axis=0, keepdims=True), axis=1, keepdims=True)

    def spread(which, phase):
        if phase == 0:
            return [push(sc.at[which, 0, 0], sc.at[which, 0, 1], sib)]
        step = (xstep, ystep, zstep)[phase - 1]
        return [push(sc.at[which, phase, 0], sc.at[which, phase, 4 - d], step(d)) for d in (1, 2, 3)]

    def collect(which, phase, copies):
        for cp in copies:
            cp.wait_recv()
        got = sc[which, phase, 0]
        for i in range(1, 2 if phase == 0 else 4):
            got = got + sc[which, phase, i]
        sc[which, phase + 1, 0] = got

    G = GROUPS1
    N = len(G)
    a, b = {}, {}
    a[0] = image(1, zb, G[0])
    a[1] = image(1, zb, G[1])

    def moments(i, m):
        rows = pl.ds(pl.multiple_of(i * 8, 8), 8)
        qr, zr = qv[rows, :], z0[rows, :]
        return m[0] + qr * qr, m[1] + qr * zr, m[2] + zr * zr

    zero = jnp.zeros((8, FQ), F32)
    mm = lax.fori_loop(0, B // 8, moments, (zero, zero, zero))
    row = lax.broadcasted_iota(jnp.int32, (8, B), 0)
    sc[0, 0, 0] = jnp.where(row == 0, total_of(mm[0]), jnp.where(row == 1, total_of(mm[1]), total_of(mm[2])))
    c = spread(0, 0)
    a[2] = image(1, zb, G[2])
    for i in range(N):
        b[i] = reduce(1, G[i], a[i])
        if i + 3 < N:
            a[i + 3] = image(1, zb, G[i + 3])
        if i >= 2:
            back(1, z1, G[i - 2], b[i - 2])
        if i < 4:
            collect(0, i, c)
            if i < 3:
                c = spread(0, i + 1)
    sc[1, 0, 0] = jnp.broadcast_to(total_of(acc[...]), (8, B))
    c = spread(1, 0)
    back(1, z1, G[N - 2], b[N - 2])
    collect(1, 0, c)
    c = spread(1, 1)
    back(1, z1, G[N - 1], b[N - 1])
    collect(1, 1, c)
    c = spread(1, 2)
    collect(1, 2, c)
    c = spread(1, 3)
    collect(1, 3, c)

    m = sc[0, 4, 0]
    m0, m1, m2 = m[0:1, 0:1], m[1:2, 0:1], m[2:3, 0:1]
    m3 = sc[1, 4, 0][0:1, 0:1]
    al0 = m0 / (m1 + DAMP * m0)
    n1 = al0 * al0 * (m2 - m1 * m1 / m0)
    beta = n1 / m0
    cz = 1.0 - DAMP * al0 + beta
    al1 = n1 / (DAMP * (n1 + beta * beta * m0) + cz * cz * m1 - 2.0 * cz * al0 * m2 + al0 * al0 * m3)

    for j in range(4):
        base = ((x + j) % 4) * R

        @pl.loop(0, R // 16)
        def _(i):
            rows = pl.ds(pl.multiple_of(j * R + i * 16, 16), 16)
            qr, z0r, z1r = qv[rows, :], z0[rows, :], z1[rows, :]
            r1 = qr - al0 * (z0r + DAMP * qr)
            d1 = r1 + beta * qr
            xv = al0 * qr + al1 * d1
            rv = r1 - al1 * (cz * z0r - al0 * z1r + DAMP * d1)
            qv[rows, :] = xv
            z0[rows, :] = rv
            to = pl.multiple_of(base + i * 16, 16)
            fin_s[pl.ds(to, 16), :] = xv.astype(BF16)
            fin_s[pl.ds(to + B, 16), :] = rv.astype(BF16)

    move_f = remote(fin_s, fin, partner, log=False)

    @pl.when(moved)
    def _():
        move_f.start()
        move_f.wait_recv()
        for i in range(FQ // B):
            cols = slice(i * B, (i + 1) * B)
            x_out[cols, :] = fin[:B, cols].astype(F32).T
            r_out[cols, :] = fin[B:, cols].astype(F32).T
        for cp in sent_moved:
            cp.wait_send()

    @pl.when(jnp.logical_not(moved))
    def _():
        for j in range(4):
            base = pl.multiple_of(((x + j) % 4) * R, R)
            z1[pl.ds(base, R), :] = qv[j * R : (j + 1) * R, :]
        for i in range(FQ // B):
            cols = slice(i * B, (i + 1) * B)
            x_out[cols, :] = z1[:, cols].T
        for j in range(4):
            base = pl.multiple_of(((x + j) % 4) * R, R)
            z1[pl.ds(base, R), :] = z0[j * R : (j + 1) * R, :]
        for i in range(FQ // B):
            cols = slice(i * B, (i + 1) * B)
            r_out[cols, :] = z1[:, cols].T

    for cp in sent:
        cp.wait_send()


def local(gate_pre, up_pre, token_weight, query_grad):
    vmem = pl.BlockSpec(memory_space=pltpu.VMEM)
    out = jax.ShapeDtypeStruct((FQ, B), F32)
    macs = 4 * T * FQ * B
    return pl.pallas_call(
        kernel,
        out_shape=(out, out),
        in_specs=[vmem] * 4,
        out_specs=(vmem, vmem),
        scratch_shapes=[
            pltpu.VMEM((T, FQ), BF16),
            pltpu.VMEM((B, FQ), BF16),
            pltpu.VMEM((2 * B, FQ), BF16),
            pltpu.VMEM((2 * B, FQ), BF16),
            pltpu.VMEM((B, FQ), F32),
            pltpu.VMEM((B, FQ), BF16),
            pltpu.VMEM((B, FQ), F32),
            pltpu.VMEM((B, FQ), BF16),
            pltpu.VMEM((B, FQ), F32),
            pltpu.VMEM((2, R, T), F32),
            pltpu.VMEM((2, 3 * R, T), BF16),
            pltpu.VMEM((2, 3, R, T), BF16),
            pltpu.VMEM((2, B, T), BF16),
            pltpu.VMEM((2, 17, 8, B), F32),
            pltpu.VMEM((8, T), F32),
            pltpu.VMEM((R, UT), F32),
            pltpu.VMEM((2, 5, 4, 8, B), F32),
            pltpu.VMEM((2 * B, FQ), BF16),
            pltpu.VMEM((2 * B, FQ), BF16),
            pltpu.SemaphoreType.DMA((NSEM,)),
            pltpu.SemaphoreType.DMA((NSEM,)),
        ],
        compiler_params=pltpu.CompilerParams(collective_id=0, has_side_effects=True, vmem_limit_bytes=56 * 2**20),
        cost_estimate=pl.CostEstimate(flops=2 * macs, bytes_accessed=8 * FQ * B * 4, transcendentals=FQ * B),
        name="cg",
    )(gate_pre, up_pre, token_weight[None, :], query_grad)


def solution(mesh):
    placed = (P("seq", "tp"), P("seq", "tp"), P("seq"), P("tp", "seq"))
    return jax.shard_map(
        local,
        mesh=mesh,
        in_specs=placed,
        out_specs=(P("tp", "seq"), P("tp", "seq")),
        check_vma=False,
    )
```

```python
import jax
import jax.numpy as jnp
from jax import lax
from jax.experimental import pallas as pl
from jax.experimental.pallas import tpu as pltpu
from jax.sharding import PartitionSpec as P

DAMP = 1.0
F32, BF16 = jnp.float32, jnp.bfloat16
MESH = pl.DeviceIdType.MESH

B = 128
FQ = 1792
R = 32
UNITS = [(0, 0), (1, 0), (3, 0), (0, 1), (0, 3), (2, 0), (0, 2), (3, 3), (1, 1), (3, 1), (1, 3), (2, 1), (2, 3), (1, 2), (3, 2), (2, 2)]
SLOT = {u: i for i, u in enumerate(UNITS)}
UT = 2 * B
T = len(UNITS) * UT
GROUPS0 = [(0, 1), (1, 3), (3, 5), (5, 7), (7, 9), (9, 11), (11, 13), (13, 15), (15, 16)]
GROUPS1 = [(0, 2), (2, 4), (4, 6), (6, 8), (8, 10), (10, 12), (12, 14), (14, 15), (15, 16)]
NSEM = 250


def kernel(gate, up, tw, q, x_out, r_out, H, nblk, hl_s, hl, qv, qb, z0, zb, z1, yown, yst, rs, sT, wb, wrow, acc, sc, dv, rn, d_s, d_r, r_s, r_r, ssem, rsem):
    s, t = lax.axis_index("seq"), lax.axis_index("tp")
    y, xh, z = s // 8, (s // 4) % 2, s % 4
    xl, k = t // 2, t % 2
    x = xh * 2 + xl

    def dev(x, y, z, k):
        return (y * 8 + (x // 2) * 4 + z, (x % 2) * 2 + k)

    def ystep(d):
        return dev(x, (y + d) % 4, z, k)

    def zstep(d):
        return dev(x, y, (z + d) % 4, k)

    def xstep(d):
        return dev((x + d) % 4, y, z, k)

    sib = dev(x, y, z, 1 - k)
    partner = dev((x + 2) % 4, y, z, 1 - k)
    moved = k != xh

    barrier = pltpu.get_barrier_semaphore()
    peers = [dev((x + d) % 4, y, z, c) for d in range(4) for c in (k, 1 - k)][1:]
    plane = [(dy, dz) for dy in range(4) for dz in range(4)][1:]
    peers += [dev(x, (y + dy) % 4, (z + dz) % 4, k) for dy, dz in plane]
    for p in peers:
        pl.semaphore_signal(barrier, inc=1, device_id=p, device_id_type=MESH)

    count = [0]
    sent, sent_moved = [], []

    def remote(src, dst, device, log=True):
        i = count[0]
        assert i < NSEM
        count[0] += 1
        cp = pltpu.make_async_remote_copy(src_ref=src, dst_ref=dst, send_sem=ssem.at[i], recv_sem=rsem.at[i], device_id=device, device_id_type=MESH)
        (sent if log else sent_moved).append(cp)
        return cp

    def push(src, dst, device):
        cp = remote(src, dst, device)
        cp.start()
        return cp

    def block(yr, zr, core=0, off=0, n=B):
        return H.at[pl.ds(SLOT[yr, zr] * UT + core * B + off, n)]

    wb[0, 0] = jnp.broadcast_to(tw[...].astype(F32) * (1.0 / T), (8, B))
    move_h = [remote(nblk.at[pl.ds(i * 32, 32)], block(0, 0, 0, i * 32, 32), partner, log=False) for i in range(4)]
    wy = []
    for i in range(4):

        @pl.loop(0, 2)
        def _(h):
            rows = pl.ds(pl.multiple_of(i * 32 + h * 16, 16), 16)
            g, u = gate[rows, :].astype(F32), up[rows, :].astype(F32)
            nblk[rows, :] = (g / (1.0 + jnp.exp(-g)) * u).astype(BF16)

        if i == 0:
            pl.semaphore_wait(barrier, len(peers))
            wy += [push(wb.at[0, 0], wb.at[0, (4 - dz) % 4 * 4 + (4 - dy) % 4], dev(x, (y + dy) % 4, (z + dz) % 4, k)) for dy, dz in plane]

        @pl.when(moved)
        def _():
            move_h[i].start()

        @pl.when(jnp.logical_not(moved))
        def _():
            block(0, 0, 0, i * 32, 32)[...] = nblk[i * 32 : (i + 1) * 32]

    def hop(yr, zr, axis, d, off, n):
        if axis == "y":
            return push(block(yr, zr, 0, off, n), block((yr - d) % 4, zr, 0, off, n), ystep(d))
        return push(block(yr, zr, 0, off, n), block(yr, (zr - d) % 4, 0, off, n), zstep(d))

    sides = [("y", 1), ("z", 1), ("y", -1), ("z", -1)]
    s1 = {}
    for i in range(4):

        @pl.when(moved)
        def _():
            move_h[i].wait_recv()

        for a, d in sides:
            s1[a, d, i] = hop(0, 0, a, d, i * 32, 32)
    relays = {}

    def relay(yr, zr):
        relays[yr, zr] = push(block(yr, zr, 0), block(yr, zr, 1), sib)

    relay(0, 0)

    for i in range(FQ // B):
        cols = slice(i * B, (i + 1) * B)
        hl_s[:, cols] = q[cols, :].T.astype(BF16)
    move_q = [remote(hl_s.at[pl.ds(i * 32, 32)], hl.at[pl.ds(i * 32, 32)], partner, log=False) for i in range(4)]

    @pl.when(moved)
    def _():
        for cp in move_q:
            cp.start()

    def s1_here(a, d, half):
        s1[a, d, 2 * half].wait_recv()
        s1[a, d, 2 * half + 1].wait_recv()

    s1_here("y", 1, 0)
    s2 = [hop(3, 0, "y", 1, 0, 64)]
    s1_here("z", 1, 0)
    s2 += [hop(0, 3, "z", 1, 0, 64)]
    s1_here("y", -1, 0)
    s1_here("y", -1, 1)
    relay(1, 0)
    s2 += [hop(1, 0, "y", -1, 64, 64)]
    s1_here("z", -1, 0)
    s1_here("z", -1, 1)
    relay(0, 1)
    s2 += [hop(0, 1, "z", -1, 64, 64)]
    s1_here("y", 1, 1)
    relay(3, 0)
    s1_here("z", 1, 1)
    relay(0, 3)
    corners = [(3, 0, "z", 1), (1, 0, "z", -1), (0, 1, "y", 1), (0, 3, "y", -1)]
    s3 = [hop(*c, 64, 64) for c in corners]
    s3 += [hop(*c, 0, 64) for c in corners]
    for cp in wy:
        cp.wait_recv()
    wp = push(wb.at[0], wb.at[1], partner)

    @pl.when(moved)
    def _():
        for cp in move_q:
            cp.wait_recv()

    @pl.when(jnp.logical_not(moved))
    def _():
        hl[...] = hl_s[...]

    bases = [pl.multiple_of(((x + j) % 4) * R, R) for j in range(4)]
    for j in range(4):
        qb[j * R : (j + 1) * R, :] = hl[pl.ds(bases[j], R), :]
    z0[...] = jnp.zeros_like(z0)
    z1[...] = jnp.zeros_like(z1)
    acc[...] = jnp.zeros_like(acc)

    def cols_of(group):
        return group[0] * UT, (group[1] - group[0]) * UT

    def image(it, p, group):
        c, n = cols_of(group)
        at = pl.ds(c, n)
        part = lax.dot_general(p[...], H[at, :], (((1,), (1,)), ((), ())), preferred_element_type=F32)
        yown[it, :, at] = part[:R]
        yst[it, :, at] = part[R:].astype(BF16)
        out = []
        for j in (2, 1, 3):
            out.append(push(yst.at[it, pl.ds((j - 1) * R, R), pl.ds(c, n)], rs.at[it, 3 - j, :, pl.ds(c, n)], xstep(j)))
        return out

    def reduce(it, group, copies):
        for cp in copies:
            cp.wait_recv()

        @pl.loop(group[0], group[1])
        def _(u):
            at = pl.ds(pl.multiple_of(u * UT, UT), UT)
            total = yown[it, :, at] + rs[it, 0, :, at].astype(F32) + rs[it, 1, :, at].astype(F32) + rs[it, 2, :, at].astype(F32)
            scaled = (total * wrow[0:1, at]).astype(BF16)
            sT[it, pl.ds(0, R), at] = scaled
            if it:
                acc[...] += total * scaled.astype(F32)

        c, n = cols_of(group)
        out = []
        for j in (2, 1, 3):
            out.append(push(sT.at[it, pl.ds(0, R), pl.ds(c, n)], sT.at[it, pl.ds((4 - j) * R, R), pl.ds(c, n)], xstep(j)))
        return out

    def back(it, zz, group, copies):
        for cp in copies:
            cp.wait_recv()

        at = pl.ds(*cols_of(group))
        zz[...] += jnp.dot(sT[it, :, at], H[at, :], preferred_element_type=F32)

    def wait_relays(group):
        for u in range(*group):
            relays[UNITS[u]].wait_recv()

    G = GROUPS0
    a, b = {}, {}

    def img(i):
        wait_relays(G[i])
        a[i] = image(0, qb, G[i])

    def red(i):
        b[i] = reduce(0, G[i], a[i])

    def bck(i):
        back(0, z0, G[i], b[i])

    img(0)
    img(1)
    for cp in s2:
        cp.wait_recv()
    relay(2, 0)
    relay(0, 2)
    img(2)
    wp.wait_recv()
    other = jnp.where(moved, 1, 0)
    for u, (yr, zr) in enumerate(UNITS):
        for c in range(2):
            wrow[0:8, u * UT + c * B : u * UT + (c + 1) * B] = wb[(other + c) % 2, zr * 4 + yr]
    for cp in s3[:4]:
        cp.wait_recv()
    s4 = [hop(2, 0, "z", 1, 0, 64), hop(2, 0, "z", -1, 0, 64)]
    s4 += [hop(3, 1, "y", 1, 64, 32), hop(1, 1, "y", -1, 96, 32), hop(3, 3, "y", 1, 64, 32), hop(1, 3, "y", -1, 96, 32)]
    red(0)
    img(3)
    red(1)
    for cp in s3[4:]:
        cp.wait_recv()
    for u in UNITS[7:11]:
        relay(*u)
    s5 = [hop(0, 2, "y", 1, 0, 64), hop(0, 2, "y", -1, 0, 64)]
    s5 += [hop(1, 3, "z", 1, 64, 32), hop(1, 1, "z", -1, 96, 32), hop(3, 3, "z", 1, 64, 32), hop(3, 1, "z", -1, 96, 32)]
    red(2)
    bck(0)
    for j in range(4):
        qv[j * R : (j + 1) * R, :] = qb[j * R : (j + 1) * R, :].astype(F32)
    red(3)
    img(4)
    img(5)
    bck(1)
    for cp in s4:
        cp.wait_recv()
    s6 = [hop(2, 3, "z", 1, 0, 32), hop(2, 1, "z", -1, 32, 32)]
    relay(2, 1)
    relay(2, 3)
    bck(2)
    red(4)
    img(6)
    red(5)
    for cp in s5:
        cp.wait_recv()
    s6 += [hop(3, 2, "y", 1, 64, 32), hop(1, 2, "y", -1, 96, 32)]
    relay(1, 2)
    relay(3, 2)
    bck(3)
    img(7)
    red(6)
    for cp in s6:
        cp.wait_recv()
    relay(2, 2)
    bck(4)
    img(8)
    red(7)
    bck(5)
    red(8)
    bck(6)
    bck(7)
    bck(8)

    zb[...] = z0[...].astype(BF16)

    def total_of(v):
        return jnp.sum(jnp.sum(v, axis=0, keepdims=True), axis=1, keepdims=True)

    def spread(which, phase):
        src = sc.at[which, phase, 0]
        if phase == 0:
            to = [(1, 1 - k), (2, k), (2, 1 - k), (3, 1 - k), (1, k), (3, k), (0, 1 - k)]
            at = [3, 2, 6, 1, 7, 5, 4]
            return [push(src, sc.at[which, 0, i], dev((x + d) % 4, y, z, c)) for (d, c), i in zip(to, at)]
        return [push(src, sc.at[which, 1, (4 - dy) % 4 * 4 + (4 - dz) % 4], dev(x, (y + dy) % 4, (z + dz) % 4, k)) for dy, dz in plane]

    def collect(which, phase, copies):
        for cp in copies:
            cp.wait_recv()
        got = sc[which, phase, 0]
        for i in range(1, 8 if phase == 0 else 16):
            got = got + sc[which, phase, i]
        sc[which, phase + 1, 0] = got

    G = GROUPS1
    N = len(G)
    a, b = {}, {}
    a[0] = image(1, zb, G[0])
    a[1] = image(1, zb, G[1])

    def moments(i, m):
        rows = pl.ds(pl.multiple_of(i * 8, 8), 8)
        qr, zr = qv[rows, :], z0[rows, :]
        return m[0] + qr * qr, m[1] + qr * zr, m[2] + zr * zr

    zero = jnp.zeros((8, FQ), F32)
    mm = lax.fori_loop(0, B // 8, moments, (zero, zero, zero))
    row = lax.broadcasted_iota(jnp.int32, (8, B), 0)
    sc[0, 0, 0] = jnp.where(row == 0, total_of(mm[0]), jnp.where(row == 1, total_of(mm[1]), total_of(mm[2])))
    c = spread(0, 0)
    a[2] = image(1, zb, G[2])
    move_d = [remote(d_s.at[pl.ds(i * 64, 64)], d_r.at[pl.ds(i * 64, 64)], partner, log=False) for i in range(2)]
    for i in range(N):
        b[i] = reduce(1, G[i], a[i])
        if i + 3 < N:
            a[i + 3] = image(1, zb, G[i + 3])
        if i >= 2:
            back(1, z1, G[i - 2], b[i - 2])
        if i < 2:
            collect(0, i, c)
            if i < 1:
                c = spread(0, i + 1)
        if i == 3:
            m = sc[0, 2, 0]
            m0, m1, m2 = m[0:1, 0:1], m[1:2, 0:1], m[2:3, 0:1]
            al0 = m0 / (m1 + DAMP * m0)
            n1 = al0 * al0 * (m2 - m1 * m1 / m0)
            beta = n1 / m0
            for j in range(4):
                base = bases[j]

                @pl.loop(0, R // 16)
                def _(h):
                    rows = pl.ds(pl.multiple_of(j * R + h * 16, 16), 16)
                    to = pl.ds(pl.multiple_of(base + h * 16, 16), 16)
                    qr = qv[rows, :]
                    d1 = qr - al0 * (z0[rows, :] + DAMP * qr) + beta * qr
                    dv[to, :] = d1
                    d_s[to, :] = d1.astype(BF16)

    sc[1, 0, 0] = jnp.broadcast_to(total_of(acc[...]), (8, B))
    c = spread(1, 0)

    @pl.when(moved)
    def _():
        for cp in move_d:
            cp.start()

    back(1, z1, G[N - 2], b[N - 2])

    @pl.when(jnp.logical_not(moved))
    def _():
        for i in range(FQ // B):
            cols = slice(i * B, (i + 1) * B)
            x_out[cols, :] = dv[:, cols].T

    collect(1, 0, c)
    c = spread(1, 1)
    back(1, z1, G[N - 1], b[N - 1])

    cz = 1.0 - DAMP * al0 + beta

    @pl.loop(0, B // 16)
    def _(i):
        rows = pl.ds(pl.multiple_of(i * 16, 16), 16)
        qr, z0r = qv[rows, :], z0[rows, :]
        r1 = qr - al0 * (z0r + DAMP * qr)
        z0[rows, :] = r1
        z1[rows, :] = cz * z0r - al0 * z1[rows, :] + DAMP * (r1 + beta * qr)

    m = sc[0, 1, 0]
    o0, o1, o2 = m[0:1, 0:1], m[1:2, 0:1], m[2:3, 0:1]
    o3 = sc[1, 1, 0][0:1, 0:1]
    keep = 1.0 - DAMP * al0
    top = keep * keep * o0 - 2.0 * al0 * keep * o1 + al0 * al0 * o2
    low = DAMP * (top + 2.0 * beta * (keep * o0 - al0 * o1) + beta * beta * o0) + cz * cz * o1 - 2.0 * cz * al0 * o2 + al0 * al0 * o3
    near = jnp.where((top > 0.0) & (low > 0.0), top / low, 1.0)
    near = jnp.where((near > 1e-6) & (near < 1e6), near, 1.0)
    W = 2 * B
    move_r = [remote(r_s.at[:, pl.ds(i * W, W)], r_r.at[:, pl.ds(i * W, W)], partner, log=False) for i in range(FQ // W)]

    @pl.when(moved)
    def _():
        for i in range(FQ // W):
            cols = slice(i * W, (i + 1) * W)
            for j in range(4):
                rows = slice(j * R, (j + 1) * R)
                r_s[pl.ds(bases[j], R), cols] = (z0[rows, cols] - near * z1[rows, cols]).astype(BF16)
            move_r[i].start()
        for cp in move_d:
            cp.wait_recv()
        for i in range(FQ // B):
            cols = slice(i * B, (i + 1) * B)
            x_out[cols, :] = d_r[:, cols].astype(F32).T

    collect(1, 1, c)
    m3 = sc[1, 2, 0][0:1, 0:1]
    al1 = n1 / (DAMP * (n1 + beta * beta * m0) + cz * cz * m1 - 2.0 * cz * al0 * m2 + al0 * al0 * m3)

    @pl.when(moved)
    def _():
        ratio = al1 / near
        for i in range(FQ // W):
            move_r[i].wait_recv()
            for c in range(i * 2, i * 2 + 2):
                cols = slice(c * B, (c + 1) * B)
                r_out[cols, :] = ratio * r_r[:, cols].astype(F32).T + (1.0 - ratio) * (x_out[cols, :] - beta * q[cols, :])

    @pl.when(jnp.logical_not(moved))
    def _():
        for i in range(FQ // B):
            cols = slice(i * B, (i + 1) * B)
            for j in range(4):
                rows = slice(j * R, (j + 1) * R)
                rn[pl.ds(bases[j], R), cols] = z0[rows, cols] - al1 * z1[rows, cols]
            r_out[cols, :] = rn[:, cols].T

    @pl.loop(0, FQ // B)
    def _(i):
        rows = pl.ds(pl.multiple_of(i * B, B), B)
        x_out[rows, :] = al0 * q[rows, :] + al1 * x_out[rows, :]

    @pl.when(moved)
    def _():
        for cp in sent_moved:
            cp.wait_send()

    for cp in sent:
        cp.wait_send()


def local(gate_pre, up_pre, token_weight, query_grad):
    vmem = pl.BlockSpec(memory_space=pltpu.VMEM)
    out = jax.ShapeDtypeStruct((FQ, B), F32)
    macs = 4 * T * FQ * B
    return pl.pallas_call(
        kernel,
        out_shape=(out, out),
        in_specs=[vmem] * 4,
        out_specs=(vmem, vmem),
        scratch_shapes=[
            pltpu.VMEM((T, FQ), BF16),
            pltpu.VMEM((B, FQ), BF16),
            pltpu.VMEM((B, FQ), BF16),
            pltpu.VMEM((B, FQ), BF16),
            pltpu.VMEM((B, FQ), F32),
            pltpu.VMEM((B, FQ), BF16),
            pltpu.VMEM((B, FQ), F32),
            pltpu.VMEM((B, FQ), BF16),
            pltpu.VMEM((B, FQ), F32),
            pltpu.VMEM((2, R, T), F32),
            pltpu.VMEM((2, 3 * R, T), BF16),
            pltpu.VMEM((2, 3, R, T), BF16),
            pltpu.VMEM((2, B, T), BF16),
            pltpu.VMEM((2, 16, 8, B), F32),
            pltpu.VMEM((8, T), F32),
            pltpu.VMEM((R, UT), F32),
            pltpu.VMEM((2, 3, 16, 8, B), F32),
            pltpu.VMEM((B, FQ), F32),
            pltpu.VMEM((B, FQ), F32),
            pltpu.VMEM((B, FQ), BF16),
            pltpu.VMEM((B, FQ), BF16),
            pltpu.VMEM((B, FQ), BF16),
            pltpu.VMEM((B, FQ), BF16),
            pltpu.SemaphoreType.DMA((NSEM,)),
            pltpu.SemaphoreType.DMA((NSEM,)),
        ],
        compiler_params=pltpu.CompilerParams(collective_id=0, has_side_effects=True, vmem_limit_bytes=56 * 2**20),
        cost_estimate=pl.CostEstimate(flops=2 * macs, bytes_accessed=8 * FQ * B * 4, transcendentals=FQ * B),
        name="cg",
    )(gate_pre, up_pre, token_weight[None, :], query_grad)


def solution(mesh):
    placed = (P("seq", "tp"), P("seq", "tp"), P("seq"), P("tp", "seq"))
    return jax.shard_map(
        local,
        mesh=mesh,
        in_specs=placed,
        out_specs=(P("tp", "seq"), P("tp", "seq")),
        check_vma=False,
    )
```

```python
import jax
import jax.numpy as jnp
from jax import lax
from jax.experimental import pallas as pl
from jax.experimental.pallas import tpu as pltpu
from jax.sharding import PartitionSpec as P

DAMP = 1.0
F32, BF16 = jnp.float32, jnp.bfloat16
MESH = pl.DeviceIdType.MESH

B = 128
FQ = 1792
R = 32
UNITS = [(0, 0), (1, 0), (3, 0), (0, 1), (0, 3), (2, 0), (0, 2), (3, 3), (1, 1), (3, 1), (1, 3), (2, 1), (2, 3), (1, 2), (3, 2), (2, 2)]
SLOT = {u: i for i, u in enumerate(UNITS)}
UT = 2 * B
T = len(UNITS) * UT
GROUPS0 = [(0, 1), (1, 3), (3, 5), (5, 7), (7, 9), (9, 11), (11, 13), (13, 15), (15, 16)]
GROUPS1 = [(0, 2), (2, 4), (4, 6), (6, 8), (8, 10), (10, 12), (12, 14), (14, 15), (15, 16)]
NSEM = 72


def kernel(gate, up, tw, q, x_out, r_out, H, nblk, hl_s, hl, qv, qb, z0, zb, z1, yown, yst, rs, sT, wb, wrow, acc, sc, dv, rn, d_s, d_r, r_s, r_r, ssem, rsem):
    s, t = lax.axis_index("seq"), lax.axis_index("tp")
    y, xh, z = s // 8, (s // 4) % 2, s % 4
    xl, k = t // 2, t % 2
    x = xh * 2 + xl

    def dev(x, y, z, k):
        return (y * 8 + (x // 2) * 4 + z, (x % 2) * 2 + k)

    def ystep(d):
        return dev(x, (y + d) % 4, z, k)

    def zstep(d):
        return dev(x, y, (z + d) % 4, k)

    def xstep(d):
        return dev((x + d) % 4, y, z, k)

    sib = dev(x, y, z, 1 - k)
    partner = dev((x + 2) % 4, y, z, 1 - k)
    moved = k != xh

    barrier = pltpu.get_barrier_semaphore()
    peers = [dev((x + d) % 4, y, z, c) for d in range(4) for c in (k, 1 - k)][1:]
    plane = [(dy, dz) for dy in range(4) for dz in range(4)][1:]
    peers += [dev(x, (y + dy) % 4, (z + dz) % 4, k) for dy, dz in plane]
    for p in peers:
        pl.semaphore_signal(barrier, inc=1, device_id=p, device_id_type=MESH)

    used = {"send": 0, "recv": 0}

    def take(kind):
        used[kind] += 1
        assert used[kind] <= NSEM
        return used[kind] - 1

    class Copies:
        def __init__(self, sends, recv=None):
            self.sends, self.recv = sends, take("recv") if recv is None else recv

        def make(self, src, dst, device):
            return pltpu.make_async_remote_copy(src_ref=src, dst_ref=dst, send_sem=ssem.at[self.sends], recv_sem=rsem.at[self.recv], device_id=device, device_id_type=MESH)

        def push(self, src, dst, device):
            self.make(src, dst, device).start()

        def wait(self, whole):
            pltpu.make_async_copy(whole, whole, rsem.at[self.recv]).wait()

    def drain(sends, whole):
        pltpu.make_async_copy(whole, whole, ssem.at[sends]).wait()

    wb[0, 0] = jnp.broadcast_to(tw[...].astype(F32) * (1.0 / T), (8, B))
    def block(yr, zr, core=0, off=0, n=B):
        return H.at[pl.ds(SLOT[yr, zr] * UT + core * B + off, n)]

    hops = take("send")

    def hop(yr, zr, axis, d, off, n, copies):
        if axis == "y":
            return copies.make(block(yr, zr, 0, off, n), block((yr - d) % 4, zr, 0, off, n), ystep(d))
        return copies.make(block(yr, zr, 0, off, n), block(yr, (zr - d) % 4, 0, off, n), zstep(d))

    h_sends = take("send")
    h_moves = [Copies(h_sends) for _ in range(4)]
    sides = [("y", 1), ("z", 1), ("y", -1), ("z", -1)]
    s1 = {(a, 1, h): Copies(hops) for a in "yz" for h in range(2)}
    s1.update({(a, -1): Copies(hops) for a in "yz"})
    w_copies = Copies(take("send"))

    def own_piece(i):
        for a, d in sides:
            hop(0, 0, a, d, i * 32, 32, s1[(a, 1, i // 2) if d == 1 else (a, -1)]).start()

    for i in range(4):

        @pl.loop(0, 2)
        def _(h):
            rows = pl.ds(pl.multiple_of(i * 32 + h * 16, 16), 16)
            g, u = gate[rows, :].astype(F32), up[rows, :].astype(F32)
            nblk[rows, :] = (g / (1.0 + jnp.exp(-g)) * u).astype(BF16)

        if i == 0:
            pl.semaphore_wait(barrier, len(peers))

        @pl.when(moved)
        def _():
            h_moves[i].push(nblk.at[pl.ds(i * 32, 32)], block(0, 0, 0, i * 32, 32), partner)

        @pl.when(jnp.logical_not(moved))
        def _():
            block(0, 0, 0, i * 32, 32)[...] = nblk[i * 32 : (i + 1) * 32]
            own_piece(i)

    for dy, dz in plane:
        w_copies.push(wb.at[0, 0], wb.at[0, (4 - dz) % 4 * 4 + (4 - dy) % 4], dev(x, (y + dy) % 4, (z + dz) % 4, k))

    @pl.when(moved)
    def _():
        for i in range(4):
            h_moves[i].wait(block(0, 0, 0, 0, 32))
            own_piece(i)

    relay_sends = take("send")
    relay_groups = [Copies(relay_sends) for _ in GROUPS0]

    def relay(yr, zr):
        g = [SLOT[yr, zr] < e for _, e in GROUPS0].index(True)
        relay_groups[g].push(block(yr, zr, 0), block(yr, zr, 1), sib)

    relay(0, 0)

    for i in range(FQ // B):
        cols = slice(i * B, (i + 1) * B)
        hl_s[:, cols] = q[cols, :].T.astype(BF16)
    q_move = Copies(take("send"))

    @pl.when(moved)
    def _():
        for i in range(4):
            q_move.push(hl_s.at[pl.ds(i * 32, 32)], hl.at[pl.ds(i * 32, 32)], partner)

    def rows_of(n):
        return H.at[pl.ds(0, n)]

    s2 = Copies(hops)
    s1["y", 1, 0].wait(rows_of(64))
    hop(3, 0, "y", 1, 0, 64, s2).start()
    s1["z", 1, 0].wait(rows_of(64))
    hop(0, 3, "z", 1, 0, 64, s2).start()
    s1["y", -1].wait(rows_of(128))
    relay(1, 0)
    hop(1, 0, "y", -1, 64, 64, s2).start()
    s1["z", -1].wait(rows_of(128))
    relay(0, 1)
    hop(0, 1, "z", -1, 64, 64, s2).start()
    s1["y", 1, 1].wait(rows_of(64))
    relay(3, 0)
    s1["z", 1, 1].wait(rows_of(64))
    relay(0, 3)
    corners = [(3, 0, "z", 1), (1, 0, "z", -1), (0, 1, "y", 1), (0, 3, "y", -1)]
    s3 = [Copies(hops), Copies(hops)]
    for c in corners:
        hop(*c, 64, 64, s3[0]).start()
    for c in corners:
        hop(*c, 0, 64, s3[1]).start()
    w_copies.wait(wb.at[0, pl.ds(1, 15)])
    w_swap = Copies(take("send"))
    w_swap.push(wb.at[0], wb.at[1], partner)

    @pl.when(moved)
    def _():
        q_move.wait(hl)

    @pl.when(jnp.logical_not(moved))
    def _():
        hl[...] = hl_s[...]

    bases = [pl.multiple_of(((x + j) % 4) * R, R) for j in range(4)]
    for j in range(4):
        qb[j * R : (j + 1) * R, :] = hl[pl.ds(bases[j], R), :]
    z0[...] = jnp.zeros_like(z0)
    z1[...] = jnp.zeros_like(z1)
    acc[...] = jnp.zeros_like(acc)

    rs_copies, ag_copies = [], []
    rs_sends, ag_sends = [take("send"), take("send")], [take("send"), take("send")]
    for it, groups in enumerate((GROUPS0, GROUPS1)):
        before = list(zip(rs_copies[0].values(), ag_copies[0].values())) if it else [(None, None)] * len(groups)
        rs_copies.append({g: Copies(rs_sends[it], a and a.recv) for g, (a, _) in zip(groups, before)})
        ag_copies.append({g: Copies(ag_sends[it], a and a.recv) for g, (_, a) in zip(groups, before)})

    def cols_of(group):
        return group[0] * UT, (group[1] - group[0]) * UT

    def image(it, p, group):
        c, n = cols_of(group)
        at = pl.ds(c, n)
        part = lax.dot_general(p[...], H[at, :], (((1,), (1,)), ((), ())), preferred_element_type=F32)
        yown[it, :, at] = part[:R]
        yst[it, :, at] = part[R:].astype(BF16)
        for j in (2, 1, 3):
            rs_copies[it][group].push(yst.at[it, pl.ds((j - 1) * R, R), at], rs.at[it, 3 - j, :, at], xstep(j))

    def reduce(it, group, between=None):
        every = pl.ds(*cols_of(group))
        rs_copies[it][group].wait(rs.at[it, :, :, every])

        @pl.loop(group[0], group[1])
        def _(u):
            at = pl.ds(pl.multiple_of(u * UT, UT), UT)
            total = yown[it, :, at] + rs[it, 0, :, at].astype(F32) + rs[it, 1, :, at].astype(F32) + rs[it, 2, :, at].astype(F32)
            scaled = (total * wrow[0:1, at]).astype(BF16)
            sT[it, pl.ds(0, R), at] = scaled
            if it:
                acc[...] += total * scaled.astype(F32)

        if between:
            between()
        for j in (2, 1, 3):
            ag_copies[it][group].push(sT.at[it, pl.ds(0, R), every], sT.at[it, pl.ds((4 - j) * R, R), every], xstep(j))

    def back(it, zz, group):
        at = pl.ds(*cols_of(group))
        ag_copies[it][group].wait(sT.at[it, pl.ds(R, 3 * R), at])
        zz[...] += jnp.dot(sT[it, :, at], H[at, :], preferred_element_type=F32)

    G = GROUPS0

    def img(i):
        lo, hi = G[i]
        relay_groups[i].wait(rows_of((hi - lo) * B))
        image(0, qb, G[i])

    def red(i):
        reduce(0, G[i])

    def bck(i):
        back(0, z0, G[i])

    img(0)
    img(1)
    s2.wait(rows_of(256))
    relay(2, 0)
    relay(0, 2)
    img(2)
    w_swap.wait(wb.at[1])
    other = jnp.where(moved, 1, 0)
    for u, (yr, zr) in enumerate(UNITS):
        for c in range(2):
            wrow[0:8, u * UT + c * B : u * UT + (c + 1) * B] = wb[(other + c) % 2, zr * 4 + yr]
    s3[0].wait(rows_of(256))
    s4, s5, s6 = Copies(hops), Copies(hops), Copies(hops)
    for c in ((2, 0, "z", 1, 0, 64), (2, 0, "z", -1, 0, 64), (3, 1, "y", 1, 64, 32), (1, 1, "y", -1, 96, 32), (3, 3, "y", 1, 64, 32), (1, 3, "y", -1, 96, 32)):
        hop(*c, s4).start()
    red(0)
    img(3)
    red(1)
    s3[1].wait(rows_of(256))
    for u in UNITS[7:11]:
        relay(*u)
    for c in ((0, 2, "y", 1, 0, 64), (0, 2, "y", -1, 0, 64), (1, 3, "z", 1, 64, 32), (1, 1, "z", -1, 96, 32), (3, 3, "z", 1, 64, 32), (3, 1, "z", -1, 96, 32)):
        hop(*c, s5).start()
    red(2)
    bck(0)
    for j in range(4):
        qv[j * R : (j + 1) * R, :] = qb[j * R : (j + 1) * R, :].astype(F32)
    red(3)
    img(4)
    img(5)
    bck(1)
    s4.wait(rows_of(256))
    hop(2, 3, "z", 1, 0, 32, s6).start()
    hop(2, 1, "z", -1, 32, 32, s6).start()
    relay(2, 1)
    relay(2, 3)
    bck(2)
    red(4)
    img(6)
    red(5)
    s5.wait(rows_of(256))
    hop(3, 2, "y", 1, 64, 32, s6).start()
    hop(1, 2, "y", -1, 96, 32, s6).start()
    relay(1, 2)
    relay(3, 2)
    bck(3)
    img(7)
    red(6)
    s6.wait(rows_of(128))
    relay(2, 2)
    bck(4)
    img(8)
    red(7)
    bck(5)
    red(8)
    bck(6)
    bck(7)
    bck(8)

    zb[...] = z0[...].astype(BF16)

    def total_of(v):
        return jnp.sum(jnp.sum(v, axis=0, keepdims=True), axis=1, keepdims=True)

    sums = {}

    def spread(which, phase):
        src, copies = sc.at[which, phase, 0], Copies(take("send"))
        sums[which, phase] = copies
        if phase == 0:
            to = [(1, 1 - k), (2, k), (2, 1 - k), (3, 1 - k), (1, k), (3, k), (0, 1 - k)]
            for (d, c), i in zip(to, [3, 2, 6, 1, 7, 5, 4]):
                copies.push(src, sc.at[which, 0, i], dev((x + d) % 4, y, z, c))
        else:
            for dy, dz in plane:
                copies.push(src, sc.at[which, 1, (4 - dy) % 4 * 4 + (4 - dz) % 4], dev(x, (y + dy) % 4, (z + dz) % 4, k))

    def collect(which, phase):
        sums[which, phase].wait(sc.at[which, phase, pl.ds(1, 7 if phase == 0 else 15)])
        got = sc[which, phase, 0]
        for i in range(1, 8 if phase == 0 else 16):
            got = got + sc[which, phase, i]
        sc[which, phase + 1, 0] = got

    G = GROUPS1
    N = len(G)
    image(1, zb, G[0])
    image(1, zb, G[1])

    def moments(i, m):
        rows = pl.ds(pl.multiple_of(i * 8, 8), 8)
        qr, zr = qv[rows, :], z0[rows, :]
        return m[0] + qr * qr, m[1] + qr * zr, m[2] + zr * zr

    zero = jnp.zeros((8, FQ), F32)
    mm = lax.fori_loop(0, B // 8, moments, (zero, zero, zero))
    row = lax.broadcasted_iota(jnp.int32, (8, B), 0)
    sc[0, 0, 0] = jnp.where(row == 0, total_of(mm[0]), jnp.where(row == 1, total_of(mm[1]), total_of(mm[2])))
    spread(0, 0)
    image(1, zb, G[2])
    d_move = Copies(take("send"))

    def ring_sum():
        sc[1, 0, 0] = jnp.broadcast_to(total_of(acc[...]), (8, B))
        spread(1, 0)

    for i in range(N):
        reduce(1, G[i], ring_sum if i == N - 1 else None)
        if i + 3 < N:
            image(1, zb, G[i + 3])
        if i >= 2:
            back(1, z1, G[i - 2])
        if i < 2:
            collect(0, i)
            if i < 1:
                spread(0, i + 1)
        if i == 3:
            m = sc[0, 2, 0]
            m0, m1, m2 = m[0:1, 0:1], m[1:2, 0:1], m[2:3, 0:1]
            al0 = m0 / (m1 + DAMP * m0)
            n1 = al0 * al0 * (m2 - m1 * m1 / m0)
            beta = n1 / m0
            for j in range(4):
                base = bases[j]

                @pl.loop(0, R // 16)
                def _(h):
                    rows = pl.ds(pl.multiple_of(j * R + h * 16, 16), 16)
                    to = pl.ds(pl.multiple_of(base + h * 16, 16), 16)
                    qr = qv[rows, :]
                    d1 = qr - al0 * (z0[rows, :] + DAMP * qr) + beta * qr
                    dv[to, :] = d1
                    d_s[to, :] = d1.astype(BF16)

    @pl.when(moved)
    def _():
        for i in range(2):
            d_move.push(d_s.at[pl.ds(i * 64, 64)], d_r.at[pl.ds(i * 64, 64)], partner)

    back(1, z1, G[N - 2])

    @pl.when(jnp.logical_not(moved))
    def _():
        for i in range(FQ // B):
            cols = slice(i * B, (i + 1) * B)
            x_out[cols, :] = dv[:, cols].T

    collect(1, 0)
    spread(1, 1)
    back(1, z1, G[N - 1])

    cz = 1.0 - DAMP * al0 + beta

    @pl.loop(0, B // 16)
    def _(i):
        rows = pl.ds(pl.multiple_of(i * 16, 16), 16)
        qr, z0r = qv[rows, :], z0[rows, :]
        r1 = qr - al0 * (z0r + DAMP * qr)
        z0[rows, :] = r1
        z1[rows, :] = cz * z0r - al0 * z1[rows, :] + DAMP * (r1 + beta * qr)

    m = sc[0, 1, 0]
    o0, o1, o2 = m[0:1, 0:1], m[1:2, 0:1], m[2:3, 0:1]
    o3 = sc[1, 1, 0][0:1, 0:1]
    keep = 1.0 - DAMP * al0
    top = keep * keep * o0 - 2.0 * al0 * keep * o1 + al0 * al0 * o2
    low = DAMP * (top + 2.0 * beta * (keep * o0 - al0 * o1) + beta * beta * o0) + cz * cz * o1 - 2.0 * cz * al0 * o2 + al0 * al0 * o3
    near = jnp.where((top > 0.0) & (low > 0.0), top / low, 1.0)
    near = jnp.where((near > 1e-6) & (near < 1e6), near, 1.0)
    W = 2 * B
    r_sends = take("send")
    r_moves = [Copies(r_sends) for _ in range(FQ // W)]

    @pl.when(moved)
    def _():
        for i in range(FQ // W):
            cols = slice(i * W, (i + 1) * W)
            for j in range(4):
                rows = slice(j * R, (j + 1) * R)
                r_s[pl.ds(bases[j], R), cols] = (z0[rows, cols] - near * z1[rows, cols]).astype(BF16)
            part = pl.ds(i * W, W)
            r_moves[i].push(r_s.at[:, part], r_r.at[:, part], partner)

    drain(hops, rows_of(1920))
    drain(relay_sends, rows_of(16 * B))
    for it in range(2):
        drain(rs_sends[it], yst.at[it])
        drain(ag_sends[it], sT.at[it, pl.ds(R, 3 * R)])
    drain(w_copies.sends, wb.at[0, pl.ds(1, 15)])
    drain(w_swap.sends, wb.at[1])
    for which, phase in sums:
        drain(sums[which, phase].sends, sc.at[which, phase, pl.ds(1, 7 if phase == 0 else 15)])

    @pl.when(jnp.logical_not(moved))
    def _():
        for i in range(FQ // B):
            cols = slice(i * B, (i + 1) * B)
            for j in range(4):
                rows = slice(j * R, (j + 1) * R)
                rn[pl.ds(bases[j], R), cols] = z0[rows, cols] - near * z1[rows, cols]
            r_out[cols, :] = rn[:, cols].T

    @pl.when(moved)
    def _():
        d_move.wait(d_r)
        for i in range(FQ // B):
            cols = slice(i * B, (i + 1) * B)
            x_out[cols, :] = d_r[:, cols].astype(F32).T

    collect(1, 1)
    m3 = sc[1, 2, 0][0:1, 0:1]
    al1 = n1 / (DAMP * (n1 + beta * beta * m0) + cz * cz * m1 - 2.0 * cz * al0 * m2 + al0 * al0 * m3)
    ratio = al1 / near

    @pl.when(jnp.logical_not(moved))
    def _():
        @pl.loop(0, FQ // B)
        def _(i):
            rows = pl.ds(pl.multiple_of(i * B, B), B)
            qr, d1 = q[rows, :], x_out[rows, :]
            r_out[rows, :] = ratio * r_out[rows, :] + (1.0 - ratio) * (d1 - beta * qr)
            x_out[rows, :] = al0 * qr + al1 * d1

    @pl.when(moved)
    def _():
        @pl.loop(0, FQ // B)
        def _(i):
            rows = pl.ds(pl.multiple_of(i * B, B), B)
            qr, d1 = q[rows, :], x_out[rows, :]
            r_out[rows, :] = (1.0 - ratio) * (d1 - beta * qr)
            x_out[rows, :] = al0 * qr + al1 * d1

        for i in range(FQ // W):
            r_moves[i].wait(r_r.at[:, pl.ds(i * W, W)])
            for c in range(i * 2, i * 2 + 2):
                cols = slice(c * B, (c + 1) * B)
                r_out[cols, :] += ratio * r_r[:, cols].astype(F32).T
        drain(h_sends, nblk)
        drain(q_move.sends, hl_s)
        drain(d_move.sends, d_s)
        drain(r_sends, r_s)


def local(gate_pre, up_pre, token_weight, query_grad):
    vmem = pl.BlockSpec(memory_space=pltpu.VMEM)
    out = jax.ShapeDtypeStruct((FQ, B), F32)
    macs = 4 * T * FQ * B
    return pl.pallas_call(
        kernel,
        out_shape=(out, out),
        in_specs=[vmem] * 4,
        out_specs=(vmem, vmem),
        scratch_shapes=[
            pltpu.VMEM((T, FQ), BF16),
            pltpu.VMEM((B, FQ), BF16),
            pltpu.VMEM((B, FQ), BF16),
            pltpu.VMEM((B, FQ), BF16),
            pltpu.VMEM((B, FQ), F32),
            pltpu.VMEM((B, FQ), BF16),
            pltpu.VMEM((B, FQ), F32),
            pltpu.VMEM((B, FQ), BF16),
            pltpu.VMEM((B, FQ), F32),
            pltpu.VMEM((2, R, T), F32),
            pltpu.VMEM((2, 3 * R, T), BF16),
            pltpu.VMEM((2, 3, R, T), BF16),
            pltpu.VMEM((2, B, T), BF16),
            pltpu.VMEM((2, 16, 8, B), F32),
            pltpu.VMEM((8, T), F32),
            pltpu.VMEM((R, UT), F32),
            pltpu.VMEM((2, 3, 16, 8, B), F32),
            pltpu.VMEM((B, FQ), F32),
            pltpu.VMEM((B, FQ), F32),
            pltpu.VMEM((B, FQ), BF16),
            pltpu.VMEM((B, FQ), BF16),
            pltpu.VMEM((B, FQ), BF16),
            pltpu.VMEM((B, FQ), BF16),
            pltpu.SemaphoreType.DMA((NSEM,)),
            pltpu.SemaphoreType.DMA((NSEM,)),
        ],
        compiler_params=pltpu.CompilerParams(collective_id=0, has_side_effects=True, vmem_limit_bytes=56 * 2**20),
        cost_estimate=pl.CostEstimate(flops=2 * macs, bytes_accessed=8 * FQ * B * 4, transcendentals=FQ * B),
        name="cg",
    )(gate_pre, up_pre, token_weight[None, :], query_grad)


def solution(mesh):
    placed = (P("seq", "tp"), P("seq", "tp"), P("seq"), P("tp", "seq"))
    return jax.shard_map(
        local,
        mesh=mesh,
        in_specs=placed,
        out_specs=(P("tp", "seq"), P("tp", "seq")),
        check_vma=False,
    )
```

```python
import jax
import jax.numpy as jnp
from jax import lax
from jax.experimental import pallas as pl
from jax.experimental.pallas import tpu as pltpu
from jax.sharding import PartitionSpec as P

DAMP = 1.0
F32, BF16 = jnp.float32, jnp.bfloat16
MESH = pl.DeviceIdType.MESH

B = 128
FQ = 1792
R = 32
UNITS = [(0, 0), (1, 0), (3, 0), (0, 1), (0, 3), (2, 0), (0, 2), (3, 3), (1, 1), (3, 1), (1, 3), (2, 1), (2, 3), (1, 2), (3, 2), (2, 2)]
SLOT = {u: i for i, u in enumerate(UNITS)}
UT = 2 * B
T = len(UNITS) * UT
GROUPS0 = [(0, 1), (1, 3), (3, 5), (5, 7), (7, 9), (9, 11), (11, 13), (13, 15), (15, 16)]
GROUPS1 = [(0, 2), (2, 4), (4, 6), (6, 8), (8, 10), (10, 12), (12, 14), (14, 15), (15, 16)]
RELAYED = 7
SEMS = {"send": 18, "recv": 65}


def kernel(gate, up, tw, q, x_out, r_out, H, nblk, hl_s, hl, qv, qb, z0, zb, z1, yown, yst, rs, sT, wb, wrow, acc, sc, dv, rn, d_r, r_s, r_r, ssem, rsem):
    s, t = lax.axis_index("seq"), lax.axis_index("tp")
    y, xh, z = s // 8, (s // 4) % 2, s % 4
    xl, k = t // 2, t % 2
    x = xh * 2 + xl

    def dev(x, y, z, k):
        return (y * 8 + (x // 2) * 4 + z, (x % 2) * 2 + k)

    def ystep(d):
        return dev(x, (y + d) % 4, z, k)

    def zstep(d):
        return dev(x, y, (z + d) % 4, k)

    def xstep(d):
        return dev((x + d) % 4, y, z, k)

    sib = dev(x, y, z, 1 - k)
    partner = dev((x + 2) % 4, y, z, 1 - k)
    moved = k != xh

    barrier = pltpu.get_barrier_semaphore()
    peers = [dev((x + d) % 4, y, z, c) for d in range(4) for c in (k, 1 - k)][1:]
    plane = [(dy, dz) for dy in range(4) for dz in range(4)][1:]
    peers += [dev(x, (y + dy) % 4, (z + dz) % 4, k) for dy, dz in plane]
    for p in peers:
        pl.semaphore_signal(barrier, inc=1, device_id=p, device_id_type=MESH)

    used = {"send": 0, "recv": 0}

    def take(kind):
        used[kind] += 1
        assert used[kind] <= SEMS[kind]
        return used[kind] - 1

    class Copies:
        def __init__(self, sends, recv=None):
            self.sends, self.recv = sends, take("recv") if recv is None else recv

        def make(self, src, dst, device):
            return pltpu.make_async_remote_copy(src_ref=src, dst_ref=dst, send_sem=ssem.at[self.sends], recv_sem=rsem.at[self.recv], device_id=device, device_id_type=MESH)

        def push(self, src, dst, device):
            self.make(src, dst, device).start()

        def wait(self, whole):
            pltpu.make_async_copy(whole, whole, rsem.at[self.recv]).wait()

    def drain(sends, whole):
        pltpu.make_async_copy(whole, whole, ssem.at[sends]).wait()

    wb[0, 0] = jnp.broadcast_to(tw[...].astype(F32) * (1.0 / T), (8, B))

    def block(yr, zr, core=0, off=0, n=B):
        return H.at[pl.ds(SLOT[yr, zr] * UT + core * B + off, n)]

    hops = take("send")

    def hop(yr, zr, axis, d, off, n, copies):
        if axis == "y":
            return copies.make(block(yr, zr, 0, off, n), block((yr - d) % 4, zr, 0, off, n), ystep(d))
        return copies.make(block(yr, zr, 0, off, n), block(yr, (zr - d) % 4, 0, off, n), zstep(d))

    h_sends = take("send")
    h_moves = [Copies(h_sends) for _ in range(4)]
    sides = [("y", 1), ("z", 1), ("y", -1), ("z", -1)]
    s1 = {(a, 1, h): Copies(hops) for a in "yz" for h in range(2)}
    s1.update({(a, -1): Copies(hops) for a in "yz"})
    w_copies = Copies(take("send"))

    def own_piece(i):
        for a, d in sides:
            hop(0, 0, a, d, i * 32, 32, s1[(a, 1, i // 2) if d == 1 else (a, -1)]).start()

    for i in range(4):

        @pl.loop(0, 2)
        def _(h):
            rows = pl.ds(pl.multiple_of(i * 32 + h * 16, 16), 16)
            g, u = gate[rows, :].astype(F32), up[rows, :].astype(F32)
            nblk[rows, :] = (g / (1.0 + jnp.exp(-g)) * u).astype(BF16)

        if i == 0:
            pl.semaphore_wait(barrier, len(peers))

        @pl.when(moved)
        def _():
            h_moves[i].push(nblk.at[pl.ds(i * 32, 32)], block(0, 0, 0, i * 32, 32), partner)

        @pl.when(jnp.logical_not(moved))
        def _():
            block(0, 0, 0, i * 32, 32)[...] = nblk[i * 32 : (i + 1) * 32]
            own_piece(i)

    for dy, dz in plane:
        w_copies.push(wb.at[0, 0], wb.at[0, (4 - dz) % 4 * 4 + (4 - dy) % 4], dev(x, (y + dy) % 4, (z + dz) % 4, k))

    @pl.when(moved)
    def _():
        for i in range(4):
            h_moves[i].wait(block(0, 0, 0, 0, 32))
            own_piece(i)

    relay_sends = take("send")
    relay_groups = [Copies(relay_sends) for _ in GROUPS0]

    def relay(yr, zr):
        g = [SLOT[yr, zr] < e for _, e in GROUPS0].index(True)
        relay_groups[g].push(block(yr, zr, 0), block(yr, zr, 1), sib)

    relay(0, 0)

    for i in range(FQ // B):
        cols = slice(i * B, (i + 1) * B)
        hl_s[:, cols] = q[cols, :].T.astype(BF16)
    q_move = Copies(take("send"))

    @pl.when(moved)
    def _():
        for i in range(4):
            q_move.push(hl_s.at[pl.ds(i * 32, 32)], hl.at[pl.ds(i * 32, 32)], partner)

    def rows_of(n):
        return H.at[pl.ds(0, n)]

    s2 = Copies(hops)
    s1["y", 1, 0].wait(rows_of(64))
    hop(3, 0, "y", 1, 0, 64, s2).start()
    s1["z", 1, 0].wait(rows_of(64))
    hop(0, 3, "z", 1, 0, 64, s2).start()
    s1["y", -1].wait(rows_of(128))
    relay(1, 0)
    hop(1, 0, "y", -1, 64, 64, s2).start()
    s1["z", -1].wait(rows_of(128))
    relay(0, 1)
    hop(0, 1, "z", -1, 64, 64, s2).start()
    s1["y", 1, 1].wait(rows_of(64))
    relay(3, 0)
    s1["z", 1, 1].wait(rows_of(64))
    relay(0, 3)
    corners = [(3, 0, "z", 1), (1, 0, "z", -1), (0, 1, "y", 1), (0, 3, "y", -1)]
    s3 = [Copies(hops), Copies(hops)]
    for c in corners:
        hop(*c, 64, 64, s3[0]).start()
    for c in corners:
        hop(*c, 0, 64, s3[1]).start()
    w_copies.wait(wb.at[0, pl.ds(1, 15)])
    w_swap = Copies(take("send"))
    w_swap.push(wb.at[0], wb.at[1], partner)

    @pl.when(moved)
    def _():
        q_move.wait(hl)

    @pl.when(jnp.logical_not(moved))
    def _():
        hl[...] = hl_s[...]

    bases = [pl.multiple_of(((x + j) % 4) * R, R) for j in range(4)]
    for j in range(4):
        qb[j * R : (j + 1) * R, :] = hl[pl.ds(bases[j], R), :]
    z0[...] = jnp.zeros_like(z0)
    z1[...] = jnp.zeros_like(z1)
    acc[...] = jnp.zeros_like(acc)

    rs_copies, ag_copies = [], []
    rs_sends, ag_sends = [take("send"), take("send")], [take("send"), take("send")]
    for it, groups in enumerate((GROUPS0, GROUPS1)):
        before = list(zip(rs_copies[0].values(), ag_copies[0].values())) if it else [(None, None)] * len(groups)
        rs_copies.append({g: Copies(rs_sends[it], a and a.recv) for g, (a, _) in zip(groups, before)})
        ag_copies.append({g: Copies(ag_sends[it], a and a.recv) for g, (_, a) in zip(groups, before)})

    onward = [{}, {g: Copies(ag_sends[1]) for g in GROUPS1[:RELAYED]}]

    def cols_of(group):
        return group[0] * UT, (group[1] - group[0]) * UT

    def image(it, p, group):
        c, n = cols_of(group)
        at = pl.ds(c, n)
        part = lax.dot_general(p[...], H[at, :], (((1,), (1,)), ((), ())), preferred_element_type=F32)
        yown[it, :, at] = part[:R]
        yst[it, :, at] = part[R:].astype(BF16)
        for j in (2, 1, 3):
            rs_copies[it][group].push(yst.at[it, pl.ds((j - 1) * R, R), at], rs.at[it, 3 - j, :, at], xstep(j))

    def reduce(it, group, between=None):
        every = pl.ds(*cols_of(group))
        rs_copies[it][group].wait(rs.at[it, :, :, every])

        @pl.loop(group[0], group[1])
        def _(u):
            at = pl.ds(pl.multiple_of(u * UT, UT), UT)
            total = yown[it, :, at] + rs[it, 0, :, at].astype(F32) + rs[it, 1, :, at].astype(F32) + rs[it, 2, :, at].astype(F32)
            scaled = (total * wrow[0:1, at]).astype(BF16)
            sT[it, pl.ds(0, R), at] = scaled
            if it:
                acc[...] += total * scaled.astype(F32)

        if between:
            between()
        for j in (1, 3) if group in onward[it] else (2, 1, 3):
            ag_copies[it][group].push(sT.at[it, pl.ds(0, R), every], sT.at[it, pl.ds((4 - j) * R, R), every], xstep(j))

    def forward(it, group):
        at = pl.ds(*cols_of(group))
        ag_copies[it][group].wait(sT.at[it, pl.ds(R, 2 * R), at])
        onward[it][group].push(sT.at[it, pl.ds(3 * R, R // 2), at], sT.at[it, pl.ds(2 * R, R // 2), at], xstep(1))
        onward[it][group].push(sT.at[it, pl.ds(R + R // 2, R // 2), at], sT.at[it, pl.ds(2 * R + R // 2, R // 2), at], xstep(3))

    def back(it, zz, group):
        at = pl.ds(*cols_of(group))
        if group in onward[it]:
            onward[it][group].wait(sT.at[it, pl.ds(2 * R, R), at])
        else:
            ag_copies[it][group].wait(sT.at[it, pl.ds(R, 3 * R), at])
        zz[...] += jnp.dot(sT[it, :, at], H[at, :], preferred_element_type=F32)

    G = GROUPS0

    def img(i):
        lo, hi = G[i]
        relay_groups[i].wait(rows_of((hi - lo) * B))
        image(0, qb, G[i])

    def red(i):
        reduce(0, G[i])

    def bck(i):
        back(0, z0, G[i])

    img(0)
    img(1)
    s2.wait(rows_of(256))
    relay(2, 0)
    relay(0, 2)
    img(2)
    w_swap.wait(wb.at[1])
    other = jnp.where(moved, 1, 0)
    for u, (yr, zr) in enumerate(UNITS):
        for c in range(2):
            wrow[0:8, u * UT + c * B : u * UT + (c + 1) * B] = wb[(other + c) % 2, zr * 4 + yr]
    s3[0].wait(rows_of(256))
    s4, s5, s6 = Copies(hops), Copies(hops), Copies(hops)
    for c in ((2, 0, "z", 1, 0, 64), (2, 0, "z", -1, 0, 64), (3, 1, "y", 1, 64, 32), (1, 1, "y", -1, 96, 32), (3, 3, "y", 1, 64, 32), (1, 3, "y", -1, 96, 32)):
        hop(*c, s4).start()
    red(0)
    img(3)
    red(1)
    s3[1].wait(rows_of(256))
    for u in UNITS[7:11]:
        relay(*u)
    for c in ((0, 2, "y", 1, 0, 64), (0, 2, "y", -1, 0, 64), (1, 3, "z", 1, 64, 32), (1, 1, "z", -1, 96, 32), (3, 3, "z", 1, 64, 32), (3, 1, "z", -1, 96, 32)):
        hop(*c, s5).start()
    red(2)
    bck(0)
    for j in range(4):
        qv[j * R : (j + 1) * R, :] = qb[j * R : (j + 1) * R, :].astype(F32)
    red(3)
    img(4)
    img(5)
    bck(1)
    s4.wait(rows_of(256))
    hop(2, 3, "z", 1, 0, 32, s6).start()
    hop(2, 1, "z", -1, 32, 32, s6).start()
    relay(2, 1)
    relay(2, 3)
    bck(2)
    red(4)
    img(6)
    red(5)
    s5.wait(rows_of(256))
    hop(3, 2, "y", 1, 64, 32, s6).start()
    hop(1, 2, "y", -1, 96, 32, s6).start()
    relay(1, 2)
    relay(3, 2)
    bck(3)
    img(7)
    red(6)
    s6.wait(rows_of(128))
    relay(2, 2)
    bck(4)
    img(8)
    red(7)
    bck(5)
    red(8)
    bck(6)
    bck(7)
    bck(8)

    zb[...] = z0[...].astype(BF16)

    def total_of(v):
        return jnp.sum(jnp.sum(v, axis=0, keepdims=True), axis=1, keepdims=True)

    sums = {}

    def spread(which, phase):
        src, copies = sc.at[which, phase, 0], Copies(take("send"))
        sums[which, phase] = copies
        if phase == 0:
            to = [(1, 1 - k), (2, k), (2, 1 - k), (3, 1 - k), (1, k), (3, k), (0, 1 - k)]
            for (d, c), i in zip(to, [3, 2, 6, 1, 7, 5, 4]):
                copies.push(src, sc.at[which, 0, i], dev((x + d) % 4, y, z, c))
        else:
            for dy, dz in plane:
                copies.push(src, sc.at[which, 1, (4 - dy) % 4 * 4 + (4 - dz) % 4], dev(x, (y + dy) % 4, (z + dz) % 4, k))

    def collect(which, phase):
        sums[which, phase].wait(sc.at[which, phase, pl.ds(1, 7 if phase == 0 else 15)])
        got = sc[which, phase, 0]
        for i in range(1, 8 if phase == 0 else 16):
            got = got + sc[which, phase, i]
        sc[which, phase + 1, 0] = got

    G = GROUPS1
    N = len(G)
    z_move = Copies(take("send"))

    def swap_rows(lo, hi):
        @pl.when(moved)
        def _():
            for j in range(lo, hi):
                z_move.push(zb.at[pl.ds(j * R, R)], d_r.at[pl.ds(bases[j], R)], partner)

    image(1, zb, G[0])
    swap_rows(0, 1)
    image(1, zb, G[1])
    swap_rows(1, 2)

    def moments(i, m):
        rows = pl.ds(pl.multiple_of(i * 8, 8), 8)
        qr, zr = qv[rows, :], z0[rows, :]
        return m[0] + qr * qr, m[1] + qr * zr, m[2] + zr * zr

    zero = jnp.zeros((8, FQ), F32)
    mm = lax.fori_loop(0, B // 8, moments, (zero, zero, zero))
    row = lax.broadcasted_iota(jnp.int32, (8, B), 0)
    sc[0, 0, 0] = jnp.where(row == 0, total_of(mm[0]), jnp.where(row == 1, total_of(mm[1]), total_of(mm[2])))
    spread(0, 0)
    image(1, zb, G[2])
    swap_rows(2, 3)
    image(1, zb, G[3])
    swap_rows(3, 4)

    def ring_sum():
        sc[1, 0, 0] = jnp.broadcast_to(total_of(acc[...]), (8, B))
        spread(1, 0)

    for i in range(N):
        reduce(1, G[i], ring_sum if i == N - 1 else None)
        if i + 4 < N:
            image(1, zb, G[i + 4])
        if 2 <= i < RELAYED + 2:
            forward(1, G[i - 2])
        if i >= 4:
            back(1, z1, G[i - 4])
        if i == 3:
            collect(0, 0)
            spread(0, 1)
        if i == 6:
            collect(0, 1)
            m = sc[0, 2, 0]
            m0, m1, m2 = m[0:1, 0:1], m[1:2, 0:1], m[2:3, 0:1]
            al0 = m0 / (m1 + DAMP * m0)
            n1 = al0 * al0 * (m2 - m1 * m1 / m0)
            beta = n1 / m0
            for j in range(4):
                base = bases[j]

                @pl.loop(0, R // 16)
                def _(h):
                    rows = pl.ds(pl.multiple_of(j * R + h * 16, 16), 16)
                    to = pl.ds(pl.multiple_of(base + h * 16, 16), 16)
                    qr = qv[rows, :]
                    d1 = qr - al0 * (z0[rows, :] + DAMP * qr) + beta * qr
                    dv[to, :] = d1

    for i in range(N - 4, N - 1):
        back(1, z1, G[i])

    @pl.when(jnp.logical_not(moved))
    def _():
        for i in range(FQ // B):
            cols = slice(i * B, (i + 1) * B)
            x_out[cols, :] = dv[:, cols].T

    @pl.when(moved)
    def _():
        z_move.wait(d_r)
        for i in range(FQ // B):
            cols = slice(i * B, (i + 1) * B)
            x_out[cols, :] = (1.0 - DAMP * al0 + beta) * q[cols, :] - al0 * d_r[:, cols].astype(F32).T

    collect(1, 0)
    spread(1, 1)
    back(1, z1, G[N - 1])

    cz = 1.0 - DAMP * al0 + beta

    @pl.loop(0, B // 16)
    def _(i):
        rows = pl.ds(pl.multiple_of(i * 16, 16), 16)
        qr, z0r = qv[rows, :], z0[rows, :]
        r1 = qr - al0 * (z0r + DAMP * qr)
        z0[rows, :] = r1
        z1[rows, :] = cz * z0r - al0 * z1[rows, :] + DAMP * (r1 + beta * qr)

    m = sc[0, 1, 0]
    o0, o1, o2 = m[0:1, 0:1], m[1:2, 0:1], m[2:3, 0:1]
    o3 = sc[1, 1, 0][0:1, 0:1]
    keep = 1.0 - DAMP * al0
    top = keep * keep * o0 - 2.0 * al0 * keep * o1 + al0 * al0 * o2
    low = DAMP * (top + 2.0 * beta * (keep * o0 - al0 * o1) + beta * beta * o0) + cz * cz * o1 - 2.0 * cz * al0 * o2 + al0 * al0 * o3
    near = jnp.where((top > 0.0) & (low > 0.0), top / low, 1.0)
    near = jnp.where((near > 1e-6) & (near < 1e6), near, 1.0)
    W = 2 * B
    r_sends = take("send")
    r_moves = [Copies(r_sends) for _ in range(FQ // W)]

    @pl.when(moved)
    def _():
        for i in range(FQ // W):
            cols = slice(i * W, (i + 1) * W)
            for j in range(4):
                rows = slice(j * R, (j + 1) * R)
                r_s[pl.ds(bases[j], R), cols] = (z0[rows, cols] - near * z1[rows, cols]).astype(BF16)
            part = pl.ds(i * W, W)
            r_moves[i].push(r_s.at[:, part], r_r.at[:, part], partner)

    drain(hops, rows_of(1920))
    drain(relay_sends, rows_of(16 * B))
    for it in range(2):
        drain(rs_sends[it], yst.at[it])
        drain(ag_sends[it], sT.at[it, pl.ds(R, 3 * R)])
    drain(w_copies.sends, wb.at[0, pl.ds(1, 15)])
    drain(w_swap.sends, wb.at[1])
    for which, phase in sums:
        drain(sums[which, phase].sends, sc.at[which, phase, pl.ds(1, 7 if phase == 0 else 15)])

    @pl.when(jnp.logical_not(moved))
    def _():
        for i in range(FQ // B):
            cols = slice(i * B, (i + 1) * B)
            for j in range(4):
                rows = slice(j * R, (j + 1) * R)
                rn[pl.ds(bases[j], R), cols] = z0[rows, cols] - near * z1[rows, cols]
            r_out[cols, :] = rn[:, cols].T

    collect(1, 1)
    m3 = sc[1, 2, 0][0:1, 0:1]
    al1 = n1 / (DAMP * (n1 + beta * beta * m0) + cz * cz * m1 - 2.0 * cz * al0 * m2 + al0 * al0 * m3)
    ratio = al1 / near

    @pl.when(jnp.logical_not(moved))
    def _():
        @pl.loop(0, FQ // B)
        def _(i):
            rows = pl.ds(pl.multiple_of(i * B, B), B)
            qr, d1 = q[rows, :], x_out[rows, :]
            r_out[rows, :] = ratio * r_out[rows, :] + (1.0 - ratio) * (d1 - beta * qr)
            x_out[rows, :] = al0 * qr + al1 * d1

    @pl.when(moved)
    def _():
        @pl.loop(0, FQ // B)
        def _(i):
            rows = pl.ds(pl.multiple_of(i * B, B), B)
            qr, d1 = q[rows, :], x_out[rows, :]
            r_out[rows, :] = (1.0 - ratio) * (d1 - beta * qr)
            x_out[rows, :] = al0 * qr + al1 * d1

        for i in range(FQ // W):
            r_moves[i].wait(r_r.at[:, pl.ds(i * W, W)])
            for c in range(i * 2, i * 2 + 2):
                cols = slice(c * B, (c + 1) * B)
                r_out[cols, :] += ratio * r_r[:, cols].astype(F32).T
        drain(h_sends, nblk)
        drain(q_move.sends, hl_s)
        drain(z_move.sends, zb)
        drain(r_sends, r_s)


def local(gate_pre, up_pre, token_weight, query_grad):
    vmem = pl.BlockSpec(memory_space=pltpu.VMEM)
    out = jax.ShapeDtypeStruct((FQ, B), F32)
    macs = 4 * T * FQ * B
    return pl.pallas_call(
        kernel,
        out_shape=(out, out),
        in_specs=[vmem] * 4,
        out_specs=(vmem, vmem),
        scratch_shapes=[
            pltpu.VMEM((T, FQ), BF16),
            pltpu.VMEM((B, FQ), BF16),
            pltpu.VMEM((B, FQ), BF16),
            pltpu.VMEM((B, FQ), BF16),
            pltpu.VMEM((B, FQ), F32),
            pltpu.VMEM((B, FQ), BF16),
            pltpu.VMEM((B, FQ), F32),
            pltpu.VMEM((B, FQ), BF16),
            pltpu.VMEM((B, FQ), F32),
            pltpu.VMEM((2, R, T), F32),
            pltpu.VMEM((2, 3 * R, T), BF16),
            pltpu.VMEM((2, 3, R, T), BF16),
            pltpu.VMEM((2, B, T), BF16),
            pltpu.VMEM((2, 16, 8, B), F32),
            pltpu.VMEM((8, T), F32),
            pltpu.VMEM((R, UT), F32),
            pltpu.VMEM((2, 3, 16, 8, B), F32),
            pltpu.VMEM((B, FQ), F32),
            pltpu.VMEM((B, FQ), F32),
            pltpu.VMEM((B, FQ), BF16),
            pltpu.VMEM((B, FQ), BF16),
            pltpu.VMEM((B, FQ), BF16),
            pltpu.SemaphoreType.DMA((SEMS["send"],)),
            pltpu.SemaphoreType.DMA((SEMS["recv"],)),
        ],
        compiler_params=pltpu.CompilerParams(collective_id=0, has_side_effects=True, vmem_limit_bytes=56 * 2**20),
        cost_estimate=pl.CostEstimate(flops=2 * macs, bytes_accessed=8 * FQ * B * 4, transcendentals=FQ * B),
        name="cg",
    )(gate_pre, up_pre, token_weight[None, :], query_grad)


def solution(mesh):
    placed = (P("seq", "tp"), P("seq", "tp"), P("seq"), P("tp", "seq"))
    return jax.shard_map(
        local,
        mesh=mesh,
        in_specs=placed,
        out_specs=(P("tp", "seq"), P("tp", "seq")),
        check_vma=False,
    )
```

```python
import jax
import jax.numpy as jnp
from jax import lax
from jax.experimental import pallas as pl
from jax.experimental.pallas import tpu as pltpu
from jax.sharding import PartitionSpec as P

DAMP = 1.0
F32, BF16 = jnp.float32, jnp.bfloat16
MESH = pl.DeviceIdType.MESH

B = 128
FQ = 1792
R = 32
UNITS = [(0, 0), (1, 0), (3, 0), (0, 1), (0, 3), (2, 0), (0, 2), (3, 3), (1, 1), (3, 1), (1, 3), (2, 1), (2, 3), (1, 2), (3, 2), (2, 2)]
SLOT = {u: i for i, u in enumerate(UNITS)}
UT = 2 * B
T = len(UNITS) * UT
GROUPS0 = [(0, 1), (1, 3), (3, 5), (5, 7), (7, 9), (9, 11), (11, 13), (13, 15), (15, 16)]
GROUPS1 = [(0, 2), (2, 4), (4, 6), (6, 8), (8, 10), (10, 12), (12, 14), (14, 15), (15, 16)]
RELAYED = 7
SEMS = {"send": 18, "recv": 72}


def kernel(gate, up, tw, q, x_out, r_out, H, nblk, hl_s, hl, qv, qb, z0, zb, z1, yown, yst, rs, ymid, yfar, sT, wb, wrow, acc, sc, dv, rn, d_r, r_s, r_r, ssem, rsem):
    s, t = lax.axis_index("seq"), lax.axis_index("tp")
    y, xh, z = s // 8, (s // 4) % 2, s % 4
    xl, k = t // 2, t % 2
    x = xh * 2 + xl

    def dev(x, y, z, k):
        return (y * 8 + (x // 2) * 4 + z, (x % 2) * 2 + k)

    def ystep(d):
        return dev(x, (y + d) % 4, z, k)

    def zstep(d):
        return dev(x, y, (z + d) % 4, k)

    def xstep(d):
        return dev((x + d) % 4, y, z, k)

    sib = dev(x, y, z, 1 - k)
    partner = dev((x + 2) % 4, y, z, 1 - k)
    moved = k != xh

    barrier = pltpu.get_barrier_semaphore()
    peers = [dev((x + d) % 4, y, z, c) for d in range(4) for c in (k, 1 - k)][1:]
    plane = [(dy, dz) for dy in range(4) for dz in range(4)][1:]
    peers += [dev(x, (y + dy) % 4, (z + dz) % 4, k) for dy, dz in plane]
    for p in peers:
        pl.semaphore_signal(barrier, inc=1, device_id=p, device_id_type=MESH)

    used = {"send": 0, "recv": 0}

    def take(kind):
        used[kind] += 1
        assert used[kind] <= SEMS[kind]
        return used[kind] - 1

    class Copies:
        def __init__(self, sends, recv=None):
            self.sends, self.recv = sends, take("recv") if recv is None else recv

        def make(self, src, dst, device):
            return pltpu.make_async_remote_copy(src_ref=src, dst_ref=dst, send_sem=ssem.at[self.sends], recv_sem=rsem.at[self.recv], device_id=device, device_id_type=MESH)

        def push(self, src, dst, device):
            self.make(src, dst, device).start()

        def wait(self, whole):
            pltpu.make_async_copy(whole, whole, rsem.at[self.recv]).wait()

    def drain(sends, whole):
        pltpu.make_async_copy(whole, whole, ssem.at[sends]).wait()

    wb[0, 0] = jnp.broadcast_to(tw[...].astype(F32) * (1.0 / T), (8, B))

    def block(yr, zr, core=0, off=0, n=B):
        return H.at[pl.ds(SLOT[yr, zr] * UT + core * B + off, n)]

    hops = take("send")

    def hop(yr, zr, axis, d, off, n, copies):
        if axis == "y":
            return copies.make(block(yr, zr, 0, off, n), block((yr - d) % 4, zr, 0, off, n), ystep(d))
        return copies.make(block(yr, zr, 0, off, n), block(yr, (zr - d) % 4, 0, off, n), zstep(d))

    h_sends = take("send")
    h_moves = [Copies(h_sends) for _ in range(4)]
    sides = [("y", 1), ("z", 1), ("y", -1), ("z", -1)]
    s1 = {(a, 1, h): Copies(hops) for a in "yz" for h in range(2)}
    s1.update({(a, -1): Copies(hops) for a in "yz"})
    w_copies = Copies(take("send"))

    def own_piece(i):
        for a, d in sides:
            hop(0, 0, a, d, i * 32, 32, s1[(a, 1, i // 2) if d == 1 else (a, -1)]).start()

    for i in range(4):

        @pl.loop(0, 2)
        def _(h):
            rows = pl.ds(pl.multiple_of(i * 32 + h * 16, 16), 16)
            g, u = gate[rows, :].astype(F32), up[rows, :].astype(F32)
            nblk[rows, :] = (g / (1.0 + jnp.exp(-g)) * u).astype(BF16)

        if i == 0:
            pl.semaphore_wait(barrier, len(peers))

        @pl.when(moved)
        def _():
            h_moves[i].push(nblk.at[pl.ds(i * 32, 32)], block(0, 0, 0, i * 32, 32), partner)

        @pl.when(jnp.logical_not(moved))
        def _():
            block(0, 0, 0, i * 32, 32)[...] = nblk[i * 32 : (i + 1) * 32]
            own_piece(i)

    for dy, dz in plane:
        w_copies.push(wb.at[0, 0], wb.at[0, (4 - dz) % 4 * 4 + (4 - dy) % 4], dev(x, (y + dy) % 4, (z + dz) % 4, k))

    @pl.when(moved)
    def _():
        for i in range(4):
            h_moves[i].wait(block(0, 0, 0, 0, 32))
            own_piece(i)

    relay_sends = take("send")
    relay_groups = [Copies(relay_sends) for _ in GROUPS0]

    def relay(yr, zr):
        g = [SLOT[yr, zr] < e for _, e in GROUPS0].index(True)
        relay_groups[g].push(block(yr, zr, 0), block(yr, zr, 1), sib)

    relay(0, 0)

    for i in range(FQ // B):
        cols = slice(i * B, (i + 1) * B)
        hl_s[:, cols] = q[cols, :].T.astype(BF16)
    q_move = Copies(take("send"))

    @pl.when(moved)
    def _():
        for i in range(4):
            q_move.push(hl_s.at[pl.ds(i * 32, 32)], hl.at[pl.ds(i * 32, 32)], partner)

    def rows_of(n):
        return H.at[pl.ds(0, n)]

    s2 = Copies(hops)
    s1["y", 1, 0].wait(rows_of(64))
    hop(3, 0, "y", 1, 0, 64, s2).start()
    s1["z", 1, 0].wait(rows_of(64))
    hop(0, 3, "z", 1, 0, 64, s2).start()
    s1["y", -1].wait(rows_of(128))
    relay(1, 0)
    hop(1, 0, "y", -1, 64, 64, s2).start()
    s1["z", -1].wait(rows_of(128))
    relay(0, 1)
    hop(0, 1, "z", -1, 64, 64, s2).start()
    s1["y", 1, 1].wait(rows_of(64))
    relay(3, 0)
    s1["z", 1, 1].wait(rows_of(64))
    relay(0, 3)
    corners = [(3, 0, "z", 1), (1, 0, "z", -1), (0, 1, "y", 1), (0, 3, "y", -1)]
    s3 = [Copies(hops), Copies(hops)]
    for c in corners:
        hop(*c, 64, 64, s3[0]).start()
    for c in corners:
        hop(*c, 0, 64, s3[1]).start()
    w_copies.wait(wb.at[0, pl.ds(1, 15)])
    w_swap = Copies(take("send"))
    w_swap.push(wb.at[0], wb.at[1], partner)

    @pl.when(moved)
    def _():
        q_move.wait(hl)

    @pl.when(jnp.logical_not(moved))
    def _():
        hl[...] = hl_s[...]

    bases = [pl.multiple_of(((x + j) % 4) * R, R) for j in range(4)]
    for j in range(4):
        qb[j * R : (j + 1) * R, :] = hl[pl.ds(bases[j], R), :]
    z0[...] = jnp.zeros_like(z0)
    z1[...] = jnp.zeros_like(z1)
    acc[...] = jnp.zeros_like(acc)

    rs_copies, ag_copies = [], []
    rs_sends, ag_sends = [take("send"), take("send")], [take("send"), take("send")]
    for it, groups in enumerate((GROUPS0, GROUPS1)):
        before = list(zip(rs_copies[0].values(), ag_copies[0].values())) if it else [(None, None)] * len(groups)
        rs_copies.append({g: Copies(rs_sends[it], a and a.recv) for g, (a, _) in zip(groups, before)})
        ag_copies.append({g: Copies(ag_sends[it], a and a.recv) for g, (_, a) in zip(groups, before)})

    onward = [{}, {g: Copies(ag_sends[1]) for g in GROUPS1[:RELAYED]}]
    far_part = {g: Copies(rs_sends[1]) for g in GROUPS1[:RELAYED]}

    def cols_of(group):
        return group[0] * UT, (group[1] - group[0]) * UT

    def image(it, p, group):
        c, n = cols_of(group)
        at = pl.ds(c, n)
        part = lax.dot_general(p[...], H[at, :], (((1,), (1,)), ((), ())), preferred_element_type=F32)
        yown[it, :, at] = part[:R]
        if group in onward[it]:
            ymid[0, :, at] = part[R : 2 * R]
            ymid[1, :, at] = part[3 * R :]
            yst[it, pl.ds(R, R), at] = part[2 * R : 3 * R].astype(BF16)
            far_part[group].push(yst.at[it, pl.ds(R, R // 2), at], yfar.at[0, :, at], xstep(1))
            far_part[group].push(yst.at[it, pl.ds(R + R // 2, R // 2), at], yfar.at[1, :, at], xstep(3))
            return
        yst[it, :, at] = part[R:].astype(BF16)
        for j in (2, 1, 3):
            rs_copies[it][group].push(yst.at[it, pl.ds((j - 1) * R, R), at], rs.at[it, 3 - j, :, at], xstep(j))

    def middle(it, group):
        at = pl.ds(*cols_of(group))
        far_part[group].wait(yfar.at[:, :, at])
        top, low = pl.ds(0, R // 2), pl.ds(R // 2, R // 2)
        yst[it, top, at] = (ymid[0, top, at] + yfar[0, :, at].astype(F32)).astype(BF16)
        yst[it, low, at] = ymid[0, low, at].astype(BF16)
        yst[it, pl.ds(2 * R, R // 2), at] = ymid[1, top, at].astype(BF16)
        yst[it, pl.ds(2 * R + R // 2, R // 2), at] = (ymid[1, low, at] + yfar[1, :, at].astype(F32)).astype(BF16)
        for j in (1, 3):
            rs_copies[it][group].push(yst.at[it, pl.ds((j - 1) * R, R), at], rs.at[it, 3 - j, :, at], xstep(j))

    def reduce(it, group, between=None):
        every = pl.ds(*cols_of(group))
        near_only = group in onward[it]
        rs_copies[it][group].wait(rs.at[it, pl.ds(0, 2 if near_only else 3), :, every])

        @pl.loop(group[0], group[1])
        def _(u):
            at = pl.ds(pl.multiple_of(u * UT, UT), UT)
            total = yown[it, :, at] + rs[it, 0, :, at].astype(F32) + rs[it, 2, :, at].astype(F32)
            if not near_only:
                total = total + rs[it, 1, :, at].astype(F32)
            scaled = (total * wrow[0:1, at]).astype(BF16)
            sT[it, pl.ds(0, R), at] = scaled
            if it:
                acc[...] += total * scaled.astype(F32)

        if between:
            between()
        for j in (1, 3) if group in onward[it] else (2, 1, 3):
            ag_copies[it][group].push(sT.at[it, pl.ds(0, R), every], sT.at[it, pl.ds((4 - j) * R, R), every], xstep(j))

    def forward(it, group):
        at = pl.ds(*cols_of(group))
        ag_copies[it][group].wait(sT.at[it, pl.ds(R, 2 * R), at])
        onward[it][group].push(sT.at[it, pl.ds(3 * R, R // 2), at], sT.at[it, pl.ds(2 * R, R // 2), at], xstep(1))
        onward[it][group].push(sT.at[it, pl.ds(R + R // 2, R // 2), at], sT.at[it, pl.ds(2 * R + R // 2, R // 2), at], xstep(3))

    def back(it, zz, group):
        at = pl.ds(*cols_of(group))
        if group in onward[it]:
            onward[it][group].wait(sT.at[it, pl.ds(2 * R, R), at])
        else:
            ag_copies[it][group].wait(sT.at[it, pl.ds(R, 3 * R), at])
        zz[...] += jnp.dot(sT[it, :, at], H[at, :], preferred_element_type=F32)

    G = GROUPS0

    def img(i):
        lo, hi = G[i]
        relay_groups[i].wait(rows_of((hi - lo) * B))
        image(0, qb, G[i])

    def red(i):
        reduce(0, G[i])

    def bck(i):
        back(0, z0, G[i])

    img(0)
    img(1)
    s2.wait(rows_of(256))
    relay(2, 0)
    relay(0, 2)
    img(2)
    w_swap.wait(wb.at[1])
    other = jnp.where(moved, 1, 0)
    for u, (yr, zr) in enumerate(UNITS):
        for c in range(2):
            wrow[0:8, u * UT + c * B : u * UT + (c + 1) * B] = wb[(other + c) % 2, zr * 4 + yr]
    s3[0].wait(rows_of(256))
    s4, s5, s6 = Copies(hops), Copies(hops), Copies(hops)
    for c in ((2, 0, "z", 1, 0, 64), (2, 0, "z", -1, 0, 64), (3, 1, "y", 1, 64, 32), (1, 1, "y", -1, 96, 32), (3, 3, "y", 1, 64, 32), (1, 3, "y", -1, 96, 32)):
        hop(*c, s4).start()
    red(0)
    img(3)
    red(1)
    s3[1].wait(rows_of(256))
    for u in UNITS[7:11]:
        relay(*u)
    for c in ((0, 2, "y", 1, 0, 64), (0, 2, "y", -1, 0, 64), (1, 3, "z", 1, 64, 32), (1, 1, "z", -1, 96, 32), (3, 3, "z", 1, 64, 32), (3, 1, "z", -1, 96, 32)):
        hop(*c, s5).start()
    red(2)
    bck(0)
    for j in range(4):
        qv[j * R : (j + 1) * R, :] = qb[j * R : (j + 1) * R, :].astype(F32)
    red(3)
    img(4)
    img(5)
    bck(1)
    s4.wait(rows_of(256))
    hop(2, 3, "z", 1, 0, 32, s6).start()
    hop(2, 1, "z", -1, 32, 32, s6).start()
    relay(2, 1)
    relay(2, 3)
    bck(2)
    red(4)
    img(6)
    red(5)
    s5.wait(rows_of(256))
    hop(3, 2, "y", 1, 64, 32, s6).start()
    hop(1, 2, "y", -1, 96, 32, s6).start()
    relay(1, 2)
    relay(3, 2)
    bck(3)
    img(7)
    red(6)
    s6.wait(rows_of(128))
    relay(2, 2)
    bck(4)
    img(8)
    red(7)
    bck(5)
    red(8)
    bck(6)
    bck(7)
    bck(8)

    zb[...] = z0[...].astype(BF16)

    def total_of(v):
        return jnp.sum(jnp.sum(v, axis=0, keepdims=True), axis=1, keepdims=True)

    sums = {}

    def spread(which, phase):
        src, copies = sc.at[which, phase, 0], Copies(take("send"))
        sums[which, phase] = copies
        if phase == 0:
            to = [(1, 1 - k), (2, k), (2, 1 - k), (3, 1 - k), (1, k), (3, k), (0, 1 - k)]
            for (d, c), i in zip(to, [3, 2, 6, 1, 7, 5, 4]):
                copies.push(src, sc.at[which, 0, i], dev((x + d) % 4, y, z, c))
        else:
            for dy, dz in plane:
                copies.push(src, sc.at[which, 1, (4 - dy) % 4 * 4 + (4 - dz) % 4], dev(x, (y + dy) % 4, (z + dz) % 4, k))

    def collect(which, phase):
        sums[which, phase].wait(sc.at[which, phase, pl.ds(1, 7 if phase == 0 else 15)])
        got = sc[which, phase, 0]
        for i in range(1, 8 if phase == 0 else 16):
            got = got + sc[which, phase, i]
        sc[which, phase + 1, 0] = got

    G = GROUPS1
    N = len(G)
    z_move = Copies(take("send"))

    def swap_rows(lo, hi):
        @pl.when(moved)
        def _():
            for j in range(lo, hi):
                z_move.push(zb.at[pl.ds(j * R, R)], d_r.at[pl.ds(bases[j], R)], partner)

    swap_rows(0, 1)
    image(1, zb, G[0])
    image(1, zb, G[1])
    swap_rows(1, 4)

    def moments(i, m):
        rows = pl.ds(pl.multiple_of(i * 8, 8), 8)
        qr, zr = qv[rows, :], z0[rows, :]
        return m[0] + qr * qr, m[1] + qr * zr, m[2] + zr * zr

    zero = jnp.zeros((8, FQ), F32)
    mm = lax.fori_loop(0, B // 8, moments, (zero, zero, zero))
    row = lax.broadcasted_iota(jnp.int32, (8, B), 0)
    sc[0, 0, 0] = jnp.where(row == 0, total_of(mm[0]), jnp.where(row == 1, total_of(mm[1]), total_of(mm[2])))
    spread(0, 0)
    image(1, zb, G[2])
    middle(1, G[0])
    image(1, zb, G[3])
    middle(1, G[1])

    def ring_sum():
        sc[1, 0, 0] = jnp.broadcast_to(total_of(acc[...]), (8, B))
        spread(1, 0)

    for i in range(N):
        if i + 2 < RELAYED:
            middle(1, G[i + 2])
        if i + 4 < N:
            image(1, zb, G[i + 4])
        reduce(1, G[i], ring_sum if i == N - 1 else None)
        if 2 <= i < RELAYED + 2:
            forward(1, G[i - 2])
        if i >= 4:
            back(1, z1, G[i - 4])
        if i == 3:
            collect(0, 0)
            spread(0, 1)
        if i == 6:
            collect(0, 1)
            m = sc[0, 2, 0]
            m0, m1, m2 = m[0:1, 0:1], m[1:2, 0:1], m[2:3, 0:1]
            al0 = m0 / (m1 + DAMP * m0)
            n1 = al0 * al0 * (m2 - m1 * m1 / m0)
            beta = n1 / m0
            for j in range(4):
                base = bases[j]

                @pl.loop(0, R // 16)
                def _(h):
                    rows = pl.ds(pl.multiple_of(j * R + h * 16, 16), 16)
                    to = pl.ds(pl.multiple_of(base + h * 16, 16), 16)
                    qr = qv[rows, :]
                    d1 = qr - al0 * (z0[rows, :] + DAMP * qr) + beta * qr
                    dv[to, :] = d1

    for i in range(N - 4, N - 1):
        back(1, z1, G[i])

    @pl.when(jnp.logical_not(moved))
    def _():
        for i in range(FQ // B):
            cols = slice(i * B, (i + 1) * B)
            x_out[cols, :] = dv[:, cols].T

    @pl.when(moved)
    def _():
        z_move.wait(d_r)
        for i in range(FQ // B):
            cols = slice(i * B, (i + 1) * B)
            x_out[cols, :] = (1.0 - DAMP * al0 + beta) * q[cols, :] - al0 * d_r[:, cols].astype(F32).T

    collect(1, 0)
    spread(1, 1)
    back(1, z1, G[N - 1])

    cz = 1.0 - DAMP * al0 + beta

    @pl.loop(0, B // 16)
    def _(i):
        rows = pl.ds(pl.multiple_of(i * 16, 16), 16)
        qr, z0r = qv[rows, :], z0[rows, :]
        r1 = qr - al0 * (z0r + DAMP * qr)
        z0[rows, :] = r1
        z1[rows, :] = cz * z0r - al0 * z1[rows, :] + DAMP * (r1 + beta * qr)

    m = sc[0, 1, 0]
    o0, o1, o2 = m[0:1, 0:1], m[1:2, 0:1], m[2:3, 0:1]
    o3 = sc[1, 1, 0][0:1, 0:1]
    keep = 1.0 - DAMP * al0
    top = keep * keep * o0 - 2.0 * al0 * keep * o1 + al0 * al0 * o2
    low = DAMP * (top + 2.0 * beta * (keep * o0 - al0 * o1) + beta * beta * o0) + cz * cz * o1 - 2.0 * cz * al0 * o2 + al0 * al0 * o3
    near = jnp.where((top > 0.0) & (low > 0.0), top / low, 1.0)
    near = jnp.where((near > 1e-6) & (near < 1e6), near, 1.0)
    W = 2 * B
    r_sends = take("send")
    r_moves = [Copies(r_sends) for _ in range(FQ // W)]

    @pl.when(moved)
    def _():
        for i in range(FQ // W):
            cols = slice(i * W, (i + 1) * W)
            for j in range(4):
                rows = slice(j * R, (j + 1) * R)
                r_s[pl.ds(bases[j], R), cols] = (z0[rows, cols] - near * z1[rows, cols]).astype(BF16)
            part = pl.ds(i * W, W)
            r_moves[i].push(r_s.at[:, part], r_r.at[:, part], partner)

    drain(hops, rows_of(1920))
    drain(relay_sends, rows_of(16 * B))
    for it in range(2):
        drain(rs_sends[it], yst.at[it])
        drain(ag_sends[it], sT.at[it, pl.ds(R, 3 * R)])
    drain(w_copies.sends, wb.at[0, pl.ds(1, 15)])
    drain(w_swap.sends, wb.at[1])
    for which, phase in sums:
        drain(sums[which, phase].sends, sc.at[which, phase, pl.ds(1, 7 if phase == 0 else 15)])

    @pl.when(jnp.logical_not(moved))
    def _():
        for i in range(FQ // B):
            cols = slice(i * B, (i + 1) * B)
            for j in range(4):
                rows = slice(j * R, (j + 1) * R)
                rn[pl.ds(bases[j], R), cols] = z0[rows, cols] - near * z1[rows, cols]
            r_out[cols, :] = rn[:, cols].T

    collect(1, 1)
    m3 = sc[1, 2, 0][0:1, 0:1]
    al1 = n1 / (DAMP * (n1 + beta * beta * m0) + cz * cz * m1 - 2.0 * cz * al0 * m2 + al0 * al0 * m3)
    ratio = al1 / near

    @pl.when(jnp.logical_not(moved))
    def _():
        @pl.loop(0, FQ // B)
        def _(i):
            rows = pl.ds(pl.multiple_of(i * B, B), B)
            qr, d1 = q[rows, :], x_out[rows, :]
            r_out[rows, :] = ratio * r_out[rows, :] + (1.0 - ratio) * (d1 - beta * qr)
            x_out[rows, :] = al0 * qr + al1 * d1

    @pl.when(moved)
    def _():
        @pl.loop(0, FQ // B)
        def _(i):
            rows = pl.ds(pl.multiple_of(i * B, B), B)
            qr, d1 = q[rows, :], x_out[rows, :]
            r_out[rows, :] = (1.0 - ratio) * (d1 - beta * qr)
            x_out[rows, :] = al0 * qr + al1 * d1

        for i in range(FQ // W):
            r_moves[i].wait(r_r.at[:, pl.ds(i * W, W)])
            for c in range(i * 2, i * 2 + 2):
                cols = slice(c * B, (c + 1) * B)
                r_out[cols, :] += ratio * r_r[:, cols].astype(F32).T
        drain(h_sends, nblk)
        drain(q_move.sends, hl_s)
        drain(z_move.sends, zb)
        drain(r_sends, r_s)


def local(gate_pre, up_pre, token_weight, query_grad):
    vmem = pl.BlockSpec(memory_space=pltpu.VMEM)
    out = jax.ShapeDtypeStruct((FQ, B), F32)
    macs = 4 * T * FQ * B
    return pl.pallas_call(
        kernel,
        out_shape=(out, out),
        in_specs=[vmem] * 4,
        out_specs=(vmem, vmem),
        scratch_shapes=[
            pltpu.VMEM((T, FQ), BF16),
            pltpu.VMEM((B, FQ), BF16),
            pltpu.VMEM((B, FQ), BF16),
            pltpu.VMEM((B, FQ), BF16),
            pltpu.VMEM((B, FQ), F32),
            pltpu.VMEM((B, FQ), BF16),
            pltpu.VMEM((B, FQ), F32),
            pltpu.VMEM((B, FQ), BF16),
            pltpu.VMEM((B, FQ), F32),
            pltpu.VMEM((2, R, T), F32),
            pltpu.VMEM((2, 3 * R, T), BF16),
            pltpu.VMEM((2, 3, R, T), BF16),
            pltpu.VMEM((2, R, T), F32),
            pltpu.VMEM((2, R // 2, T), BF16),
            pltpu.VMEM((2, B, T), BF16),
            pltpu.VMEM((2, 16, 8, B), F32),
            pltpu.VMEM((8, T), F32),
            pltpu.VMEM((R, UT), F32),
            pltpu.VMEM((2, 3, 16, 8, B), F32),
            pltpu.VMEM((B, FQ), F32),
            pltpu.VMEM((B, FQ), F32),
            pltpu.VMEM((B, FQ), BF16),
            pltpu.VMEM((B, FQ), BF16),
            pltpu.VMEM((B, FQ), BF16),
            pltpu.SemaphoreType.DMA((SEMS["send"],)),
            pltpu.SemaphoreType.DMA((SEMS["recv"],)),
        ],
        compiler_params=pltpu.CompilerParams(collective_id=0, has_side_effects=True, vmem_limit_bytes=56 * 2**20),
        cost_estimate=pl.CostEstimate(flops=2 * macs, bytes_accessed=8 * FQ * B * 4, transcendentals=FQ * B),
        name="cg",
    )(gate_pre, up_pre, token_weight[None, :], query_grad)


def solution(mesh):
    placed = (P("seq", "tp"), P("seq", "tp"), P("seq"), P("tp", "seq"))
    return jax.shard_map(
        local,
        mesh=mesh,
        in_specs=placed,
        out_specs=(P("tp", "seq"), P("tp", "seq")),
        check_vma=False,
    )
```

```python
import jax
import jax.numpy as jnp
from jax import lax
from jax.experimental import pallas as pl
from jax.experimental.pallas import tpu as pltpu
from jax.sharding import PartitionSpec as P

DAMP = 1.0
F32, BF16 = jnp.float32, jnp.bfloat16
MESH = pl.DeviceIdType.MESH

B = 128
FQ = 1792
R = 32
UNITS = [(0, 0), (1, 0), (3, 0), (0, 1), (0, 3), (2, 0), (0, 2), (3, 3), (1, 1), (3, 1), (1, 3), (2, 1), (2, 3), (1, 2), (3, 2), (2, 2)]
SLOT = {u: i for i, u in enumerate(UNITS)}
UT = 2 * B
T = len(UNITS) * UT
GROUPS0 = [(0, 1), (1, 3), (3, 5), (5, 7), (7, 9), (9, 11), (11, 13), (13, 15), (15, 16)]
GROUPS1 = [(0, 1), (1, 3), (3, 5), (5, 7), (7, 9), (9, 11), (11, 13), (13, 15), (15, 16)]
RELAYED = 7
SEMS = {"send": 18, "recv": 72}


def kernel(gate, up, tw, q, x_out, r_out, H, nblk, hl_s, hl, qv, qb, z0, zb, z1, yown, yst, rs, ymid, yfar, sT, wb, wrow, acc, sc, dv, rn, d_r, r_s, r_r, ssem, rsem):
    s, t = lax.axis_index("seq"), lax.axis_index("tp")
    y, xh, z = s // 8, (s // 4) % 2, s % 4
    xl, k = t // 2, t % 2
    x = xh * 2 + xl

    def dev(x, y, z, k):
        return (y * 8 + (x // 2) * 4 + z, (x % 2) * 2 + k)

    def ystep(d):
        return dev(x, (y + d) % 4, z, k)

    def zstep(d):
        return dev(x, y, (z + d) % 4, k)

    def xstep(d):
        return dev((x + d) % 4, y, z, k)

    sib = dev(x, y, z, 1 - k)
    partner = dev((x + 2) % 4, y, z, 1 - k)
    moved = k != xh

    barrier = pltpu.get_barrier_semaphore()
    peers = [dev((x + d) % 4, y, z, c) for d in range(4) for c in (k, 1 - k)][1:]
    plane = [(dy, dz) for dy in range(4) for dz in range(4)][1:]
    peers += [dev(x, (y + dy) % 4, (z + dz) % 4, k) for dy, dz in plane]
    for p in peers:
        pl.semaphore_signal(barrier, inc=1, device_id=p, device_id_type=MESH)

    used = {"send": 0, "recv": 0}

    def take(kind):
        used[kind] += 1
        assert used[kind] <= SEMS[kind]
        return used[kind] - 1

    class Copies:
        def __init__(self, sends, recv=None):
            self.sends, self.recv = sends, take("recv") if recv is None else recv

        def make(self, src, dst, device):
            return pltpu.make_async_remote_copy(src_ref=src, dst_ref=dst, send_sem=ssem.at[self.sends], recv_sem=rsem.at[self.recv], device_id=device, device_id_type=MESH)

        def push(self, src, dst, device):
            self.make(src, dst, device).start()

        def wait(self, whole):
            pltpu.make_async_copy(whole, whole, rsem.at[self.recv]).wait()

    def drain(sends, whole):
        pltpu.make_async_copy(whole, whole, ssem.at[sends]).wait()

    wb[0, 0] = jnp.broadcast_to(tw[...].astype(F32) * (1.0 / T), (8, B))

    def block(yr, zr, core=0, off=0, n=B):
        return H.at[pl.ds(SLOT[yr, zr] * UT + core * B + off, n)]

    hops = take("send")

    def hop(yr, zr, axis, d, off, n, copies):
        if axis == "y":
            return copies.make(block(yr, zr, 0, off, n), block((yr - d) % 4, zr, 0, off, n), ystep(d))
        return copies.make(block(yr, zr, 0, off, n), block(yr, (zr - d) % 4, 0, off, n), zstep(d))

    h_sends = take("send")
    h_moves = [Copies(h_sends) for _ in range(4)]
    sides = [("y", 1), ("z", 1), ("y", -1), ("z", -1)]
    s1 = {(a, 1, h): Copies(hops) for a in "yz" for h in range(2)}
    s1.update({(a, -1): Copies(hops) for a in "yz"})
    w_copies = Copies(take("send"))

    def own_piece(i):
        for a, d in sides:
            hop(0, 0, a, d, i * 32, 32, s1[(a, 1, i // 2) if d == 1 else (a, -1)]).start()

    for i in range(4):

        @pl.loop(0, 2)
        def _(h):
            rows = pl.ds(pl.multiple_of(i * 32 + h * 16, 16), 16)
            g, u = gate[rows, :].astype(F32), up[rows, :].astype(F32)
            nblk[rows, :] = (g / (1.0 + jnp.exp(-g)) * u).astype(BF16)

        if i == 0:
            pl.semaphore_wait(barrier, len(peers))

        @pl.when(moved)
        def _():
            h_moves[i].push(nblk.at[pl.ds(i * 32, 32)], block(0, 0, 0, i * 32, 32), partner)

        @pl.when(jnp.logical_not(moved))
        def _():
            block(0, 0, 0, i * 32, 32)[...] = nblk[i * 32 : (i + 1) * 32]
            own_piece(i)

    for dy, dz in plane:
        w_copies.push(wb.at[0, 0], wb.at[0, (4 - dz) % 4 * 4 + (4 - dy) % 4], dev(x, (y + dy) % 4, (z + dz) % 4, k))

    @pl.when(moved)
    def _():
        for i in range(4):
            h_moves[i].wait(block(0, 0, 0, 0, 32))
            own_piece(i)

    relay_sends = take("send")
    relay_groups = [Copies(relay_sends) for _ in GROUPS0]

    def relay(yr, zr):
        g = [SLOT[yr, zr] < e for _, e in GROUPS0].index(True)
        relay_groups[g].push(block(yr, zr, 0), block(yr, zr, 1), sib)

    relay(0, 0)

    for i in range(FQ // B):
        cols = slice(i * B, (i + 1) * B)
        hl_s[:, cols] = q[cols, :].T.astype(BF16)
    q_move = Copies(take("send"))

    @pl.when(moved)
    def _():
        for i in range(4):
            q_move.push(hl_s.at[pl.ds(i * 32, 32)], hl.at[pl.ds(i * 32, 32)], partner)

    def rows_of(n):
        return H.at[pl.ds(0, n)]

    s2 = Copies(hops)
    s1["y", 1, 0].wait(rows_of(64))
    hop(3, 0, "y", 1, 0, 64, s2).start()
    s1["z", 1, 0].wait(rows_of(64))
    hop(0, 3, "z", 1, 0, 64, s2).start()
    s1["y", -1].wait(rows_of(128))
    relay(1, 0)
    hop(1, 0, "y", -1, 64, 64, s2).start()
    s1["z", -1].wait(rows_of(128))
    relay(0, 1)
    hop(0, 1, "z", -1, 64, 64, s2).start()
    s1["y", 1, 1].wait(rows_of(64))
    relay(3, 0)
    s1["z", 1, 1].wait(rows_of(64))
    relay(0, 3)
    corners = [(3, 0, "z", 1), (1, 0, "z", -1), (0, 1, "y", 1), (0, 3, "y", -1)]
    s3 = [Copies(hops), Copies(hops)]
    for c in corners:
        hop(*c, 64, 64, s3[0]).start()
    for c in corners:
        hop(*c, 0, 64, s3[1]).start()
    w_copies.wait(wb.at[0, pl.ds(1, 15)])
    w_swap = Copies(take("send"))
    w_swap.push(wb.at[0], wb.at[1], partner)

    @pl.when(moved)
    def _():
        q_move.wait(hl)

    @pl.when(jnp.logical_not(moved))
    def _():
        hl[...] = hl_s[...]

    bases = [pl.multiple_of(((x + j) % 4) * R, R) for j in range(4)]
    for j in range(4):
        qb[j * R : (j + 1) * R, :] = hl[pl.ds(bases[j], R), :]
    z0[...] = jnp.zeros_like(z0)
    z1[...] = jnp.zeros_like(z1)
    acc[...] = jnp.zeros_like(acc)

    rs_copies, ag_copies = [], []
    rs_sends, ag_sends = [take("send"), take("send")], [take("send"), take("send")]
    for it, groups in enumerate((GROUPS0, GROUPS1)):
        before = list(zip(rs_copies[0].values(), ag_copies[0].values())) if it else [(None, None)] * len(groups)
        rs_copies.append({g: Copies(rs_sends[it], a and a.recv) for g, (a, _) in zip(groups, before)})
        ag_copies.append({g: Copies(ag_sends[it], a and a.recv) for g, (_, a) in zip(groups, before)})

    onward = [{}, {g: Copies(ag_sends[1]) for g in GROUPS1[:RELAYED]}]
    far_part = {g: Copies(rs_sends[1]) for g in GROUPS1[:RELAYED]}

    def cols_of(group):
        return group[0] * UT, (group[1] - group[0]) * UT

    def image(it, p, group):
        c, n = cols_of(group)
        at = pl.ds(c, n)
        part = lax.dot_general(p[...], H[at, :], (((1,), (1,)), ((), ())), preferred_element_type=F32)
        yown[it, :, at] = part[:R]
        if group in onward[it]:
            ymid[0, :, at] = part[R : 2 * R]
            ymid[1, :, at] = part[3 * R :]
            yst[it, pl.ds(R, R), at] = part[2 * R : 3 * R].astype(BF16)
            far_part[group].push(yst.at[it, pl.ds(R, R // 2), at], yfar.at[0, :, at], xstep(1))
            far_part[group].push(yst.at[it, pl.ds(R + R // 2, R // 2), at], yfar.at[1, :, at], xstep(3))
            return
        yst[it, :, at] = part[R:].astype(BF16)
        for j in (2, 1, 3):
            rs_copies[it][group].push(yst.at[it, pl.ds((j - 1) * R, R), at], rs.at[it, 3 - j, :, at], xstep(j))

    def middle(it, group):
        at = pl.ds(*cols_of(group))
        far_part[group].wait(yfar.at[:, :, at])
        top, low = pl.ds(0, R // 2), pl.ds(R // 2, R // 2)
        yst[it, top, at] = (ymid[0, top, at] + yfar[0, :, at].astype(F32)).astype(BF16)
        yst[it, low, at] = ymid[0, low, at].astype(BF16)
        yst[it, pl.ds(2 * R, R // 2), at] = ymid[1, top, at].astype(BF16)
        yst[it, pl.ds(2 * R + R // 2, R // 2), at] = (ymid[1, low, at] + yfar[1, :, at].astype(F32)).astype(BF16)
        for j in (1, 3):
            rs_copies[it][group].push(yst.at[it, pl.ds((j - 1) * R, R), at], rs.at[it, 3 - j, :, at], xstep(j))

    def reduce(it, group, between=None):
        every = pl.ds(*cols_of(group))
        near_only = group in onward[it]
        rs_copies[it][group].wait(rs.at[it, pl.ds(0, 2 if near_only else 3), :, every])

        @pl.loop(group[0], group[1])
        def _(u):
            at = pl.ds(pl.multiple_of(u * UT, UT), UT)
            total = yown[it, :, at] + rs[it, 0, :, at].astype(F32) + rs[it, 2, :, at].astype(F32)
            if not near_only:
                total = total + rs[it, 1, :, at].astype(F32)
            scaled = (total * wrow[0:1, at]).astype(BF16)
            sT[it, pl.ds(0, R), at] = scaled
            if it:
                acc[...] += total * scaled.astype(F32)

        if between:
            between()
        for j in (1, 3) if group in onward[it] else (2, 1, 3):
            ag_copies[it][group].push(sT.at[it, pl.ds(0, R), every], sT.at[it, pl.ds((4 - j) * R, R), every], xstep(j))

    def forward(it, group):
        at = pl.ds(*cols_of(group))
        ag_copies[it][group].wait(sT.at[it, pl.ds(R, 2 * R), at])
        onward[it][group].push(sT.at[it, pl.ds(3 * R, R // 2), at], sT.at[it, pl.ds(2 * R, R // 2), at], xstep(1))
        onward[it][group].push(sT.at[it, pl.ds(R + R // 2, R // 2), at], sT.at[it, pl.ds(2 * R + R // 2, R // 2), at], xstep(3))

    def back(it, zz, group):
        at = pl.ds(*cols_of(group))
        if group in onward[it]:
            onward[it][group].wait(sT.at[it, pl.ds(2 * R, R), at])
        else:
            ag_copies[it][group].wait(sT.at[it, pl.ds(R, 3 * R), at])
        zz[...] += jnp.dot(sT[it, :, at], H[at, :], preferred_element_type=F32)

    G = GROUPS0

    def img(i):
        lo, hi = G[i]
        relay_groups[i].wait(rows_of((hi - lo) * B))
        image(0, qb, G[i])

    def red(i):
        reduce(0, G[i])

    def bck(i):
        back(0, z0, G[i])

    img(0)
    img(1)
    s2.wait(rows_of(256))
    relay(2, 0)
    relay(0, 2)
    img(2)
    w_swap.wait(wb.at[1])
    other = jnp.where(moved, 1, 0)
    for u, (yr, zr) in enumerate(UNITS):
        for c in range(2):
            wrow[0:8, u * UT + c * B : u * UT + (c + 1) * B] = wb[(other + c) % 2, zr * 4 + yr]
    s3[0].wait(rows_of(256))
    s4, s5, s6 = Copies(hops), Copies(hops), Copies(hops)
    for c in ((2, 0, "z", 1, 0, 64), (2, 0, "z", -1, 0, 64), (3, 1, "y", 1, 64, 32), (1, 1, "y", -1, 96, 32), (3, 3, "y", 1, 64, 32), (1, 3, "y", -1, 96, 32)):
        hop(*c, s4).start()
    red(0)
    img(3)
    red(1)
    s3[1].wait(rows_of(256))
    for u in UNITS[7:11]:
        relay(*u)
    for c in ((0, 2, "y", 1, 0, 64), (0, 2, "y", -1, 0, 64), (1, 3, "z", 1, 64, 32), (1, 1, "z", -1, 96, 32), (3, 3, "z", 1, 64, 32), (3, 1, "z", -1, 96, 32)):
        hop(*c, s5).start()
    red(2)
    for j in range(4):
        qv[j * R : (j + 1) * R, :] = qb[j * R : (j + 1) * R, :].astype(F32)
    red(3)
    img(4)
    bck(0)
    img(5)
    bck(1)
    s4.wait(rows_of(256))
    hop(2, 3, "z", 1, 0, 32, s6).start()
    hop(2, 1, "z", -1, 32, 32, s6).start()
    relay(2, 1)
    relay(2, 3)
    bck(2)
    red(4)
    img(6)
    red(5)
    s5.wait(rows_of(256))
    hop(3, 2, "y", 1, 64, 32, s6).start()
    hop(1, 2, "y", -1, 96, 32, s6).start()
    relay(1, 2)
    relay(3, 2)
    bck(3)
    bck(4)
    red(6)
    img(7)
    s6.wait(rows_of(128))
    relay(2, 2)
    bck(5)
    img(8)
    red(7)
    bck(6)
    red(8)
    bck(7)
    bck(8)

    zb[...] = z0[...].astype(BF16)

    def total_of(v):
        return jnp.sum(jnp.sum(v, axis=0, keepdims=True), axis=1, keepdims=True)

    sums = {}

    def spread(which, phase):
        src, copies = sc.at[which, phase, 0], Copies(take("send"))
        sums[which, phase] = copies
        if phase == 0:
            to = [(1, 1 - k), (2, k), (2, 1 - k), (3, 1 - k), (1, k), (3, k), (0, 1 - k)]
            for (d, c), i in zip(to, [3, 2, 6, 1, 7, 5, 4]):
                copies.push(src, sc.at[which, 0, i], dev((x + d) % 4, y, z, c))
        else:
            for dy, dz in plane:
                copies.push(src, sc.at[which, 1, (4 - dy) % 4 * 4 + (4 - dz) % 4], dev(x, (y + dy) % 4, (z + dz) % 4, k))

    def collect(which, phase):
        sums[which, phase].wait(sc.at[which, phase, pl.ds(1, 7 if phase == 0 else 15)])
        got = sc[which, phase, 0]
        for i in range(1, 8 if phase == 0 else 16):
            got = got + sc[which, phase, i]
        sc[which, phase + 1, 0] = got

    G = GROUPS1
    N = len(G)
    z_move = Copies(take("send"))

    def swap_rows(lo, hi):
        @pl.when(moved)
        def _():
            for j in range(lo, hi):
                z_move.push(zb.at[pl.ds(j * R, R)], d_r.at[pl.ds(bases[j], R)], partner)

    swap_rows(0, 1)
    image(1, zb, G[0])
    image(1, zb, G[1])
    swap_rows(1, 4)

    def moments(i, m):
        rows = pl.ds(pl.multiple_of(i * 8, 8), 8)
        qr, zr = qv[rows, :], z0[rows, :]
        return m[0] + qr * qr, m[1] + qr * zr, m[2] + zr * zr

    zero = jnp.zeros((8, FQ), F32)
    mm = lax.fori_loop(0, B // 8, moments, (zero, zero, zero))
    row = lax.broadcasted_iota(jnp.int32, (8, B), 0)
    sc[0, 0, 0] = jnp.where(row == 0, total_of(mm[0]), jnp.where(row == 1, total_of(mm[1]), total_of(mm[2])))
    spread(0, 0)
    image(1, zb, G[2])
    middle(1, G[0])
    image(1, zb, G[3])
    middle(1, G[1])

    def ring_sum():
        sc[1, 0, 0] = jnp.broadcast_to(total_of(acc[...]), (8, B))
        spread(1, 0)

    for i in range(N):
        if i + 2 < RELAYED:
            middle(1, G[i + 2])
        if i + 4 < N:
            image(1, zb, G[i + 4])
        reduce(1, G[i], ring_sum if i == N - 1 else None)
        if 2 <= i < RELAYED + 2:
            forward(1, G[i - 2])
        if i >= 4:
            back(1, z1, G[i - 4])
        if i == 3:
            collect(0, 0)
            spread(0, 1)
        if i == 6:
            collect(0, 1)
            m = sc[0, 2, 0]
            m0, m1, m2 = m[0:1, 0:1], m[1:2, 0:1], m[2:3, 0:1]
            al0 = m0 / (m1 + DAMP * m0)
            n1 = al0 * al0 * (m2 - m1 * m1 / m0)
            beta = n1 / m0
            for j in range(4):
                base = bases[j]

                @pl.loop(0, R // 16)
                def _(h):
                    rows = pl.ds(pl.multiple_of(j * R + h * 16, 16), 16)
                    to = pl.ds(pl.multiple_of(base + h * 16, 16), 16)
                    qr = qv[rows, :]
                    d1 = qr - al0 * (z0[rows, :] + DAMP * qr) + beta * qr
                    dv[to, :] = d1

    for i in range(N - 4, N - 1):
        back(1, z1, G[i])

    @pl.when(jnp.logical_not(moved))
    def _():
        for i in range(FQ // B):
            cols = slice(i * B, (i + 1) * B)
            x_out[cols, :] = dv[:, cols].T

    @pl.when(moved)
    def _():
        z_move.wait(d_r)
        for i in range(FQ // B):
            cols = slice(i * B, (i + 1) * B)
            x_out[cols, :] = (1.0 - DAMP * al0 + beta) * q[cols, :] - al0 * d_r[:, cols].astype(F32).T

    collect(1, 0)
    spread(1, 1)
    back(1, z1, G[N - 1])

    cz = 1.0 - DAMP * al0 + beta

    @pl.loop(0, B // 16)
    def _(i):
        rows = pl.ds(pl.multiple_of(i * 16, 16), 16)
        qr, z0r = qv[rows, :], z0[rows, :]
        r1 = qr - al0 * (z0r + DAMP * qr)
        z0[rows, :] = r1
        z1[rows, :] = cz * z0r - al0 * z1[rows, :] + DAMP * (r1 + beta * qr)

    m = sc[0, 1, 0]
    o0, o1, o2 = m[0:1, 0:1], m[1:2, 0:1], m[2:3, 0:1]
    o3 = sc[1, 1, 0][0:1, 0:1]
    keep = 1.0 - DAMP * al0
    top = keep * keep * o0 - 2.0 * al0 * keep * o1 + al0 * al0 * o2
    low = DAMP * (top + 2.0 * beta * (keep * o0 - al0 * o1) + beta * beta * o0) + cz * cz * o1 - 2.0 * cz * al0 * o2 + al0 * al0 * o3
    near = jnp.where((top > 0.0) & (low > 0.0), top / low, 1.0)
    near = jnp.where((near > 1e-6) & (near < 1e6), near, 1.0)
    W = 2 * B
    r_sends = take("send")
    r_moves = [Copies(r_sends) for _ in range(FQ // W)]

    @pl.when(moved)
    def _():
        for i in range(FQ // W):
            cols = slice(i * W, (i + 1) * W)
            for j in range(4):
                rows = slice(j * R, (j + 1) * R)
                r_s[pl.ds(bases[j], R), cols] = (z0[rows, cols] - near * z1[rows, cols]).astype(BF16)
            part = pl.ds(i * W, W)
            r_moves[i].push(r_s.at[:, part], r_r.at[:, part], partner)

    drain(hops, rows_of(1920))
    drain(relay_sends, rows_of(16 * B))
    for it in range(2):
        drain(rs_sends[it], yst.at[it])
        drain(ag_sends[it], sT.at[it, pl.ds(R, 3 * R)])
    drain(w_copies.sends, wb.at[0, pl.ds(1, 15)])
    drain(w_swap.sends, wb.at[1])
    for which, phase in sums:
        drain(sums[which, phase].sends, sc.at[which, phase, pl.ds(1, 7 if phase == 0 else 15)])

    @pl.when(jnp.logical_not(moved))
    def _():
        for i in range(FQ // B):
            cols = slice(i * B, (i + 1) * B)
            for j in range(4):
                rows = slice(j * R, (j + 1) * R)
                rn[pl.ds(bases[j], R), cols] = z0[rows, cols] - near * z1[rows, cols]
            r_out[cols, :] = rn[:, cols].T

    collect(1, 1)
    m3 = sc[1, 2, 0][0:1, 0:1]
    al1 = n1 / (DAMP * (n1 + beta * beta * m0) + cz * cz * m1 - 2.0 * cz * al0 * m2 + al0 * al0 * m3)
    ratio = al1 / near

    @pl.when(jnp.logical_not(moved))
    def _():
        @pl.loop(0, FQ // B)
        def _(i):
            rows = pl.ds(pl.multiple_of(i * B, B), B)
            qr, d1 = q[rows, :], x_out[rows, :]
            r_out[rows, :] = ratio * r_out[rows, :] + (1.0 - ratio) * (d1 - beta * qr)
            x_out[rows, :] = al0 * qr + al1 * d1

    @pl.when(moved)
    def _():
        @pl.loop(0, FQ // B)
        def _(i):
            rows = pl.ds(pl.multiple_of(i * B, B), B)
            qr, d1 = q[rows, :], x_out[rows, :]
            r_out[rows, :] = (1.0 - ratio) * (d1 - beta * qr)
            x_out[rows, :] = al0 * qr + al1 * d1

        for i in range(FQ // W):
            r_moves[i].wait(r_r.at[:, pl.ds(i * W, W)])
            for c in range(i * 2, i * 2 + 2):
                cols = slice(c * B, (c + 1) * B)
                r_out[cols, :] += ratio * r_r[:, cols].astype(F32).T
        drain(h_sends, nblk)
        drain(q_move.sends, hl_s)
        drain(z_move.sends, zb)
        drain(r_sends, r_s)


def local(gate_pre, up_pre, token_weight, query_grad):
    vmem = pl.BlockSpec(memory_space=pltpu.VMEM)
    out = jax.ShapeDtypeStruct((FQ, B), F32)
    macs = 4 * T * FQ * B
    return pl.pallas_call(
        kernel,
        out_shape=(out, out),
        in_specs=[vmem] * 4,
        out_specs=(vmem, vmem),
        scratch_shapes=[
            pltpu.VMEM((T, FQ), BF16),
            pltpu.VMEM((B, FQ), BF16),
            pltpu.VMEM((B, FQ), BF16),
            pltpu.VMEM((B, FQ), BF16),
            pltpu.VMEM((B, FQ), F32),
            pltpu.VMEM((B, FQ), BF16),
            pltpu.VMEM((B, FQ), F32),
            pltpu.VMEM((B, FQ), BF16),
            pltpu.VMEM((B, FQ), F32),
            pltpu.VMEM((2, R, T), F32),
            pltpu.VMEM((2, 3 * R, T), BF16),
            pltpu.VMEM((2, 3, R, T), BF16),
            pltpu.VMEM((2, R, T), F32),
            pltpu.VMEM((2, R // 2, T), BF16),
            pltpu.VMEM((2, B, T), BF16),
            pltpu.VMEM((2, 16, 8, B), F32),
            pltpu.VMEM((8, T), F32),
            pltpu.VMEM((R, UT), F32),
            pltpu.VMEM((2, 3, 16, 8, B), F32),
            pltpu.VMEM((B, FQ), F32),
            pltpu.VMEM((B, FQ), F32),
            pltpu.VMEM((B, FQ), BF16),
            pltpu.VMEM((B, FQ), BF16),
            pltpu.VMEM((B, FQ), BF16),
            pltpu.SemaphoreType.DMA((SEMS["send"],)),
            pltpu.SemaphoreType.DMA((SEMS["recv"],)),
        ],
        compiler_params=pltpu.CompilerParams(collective_id=0, has_side_effects=True, vmem_limit_bytes=56 * 2**20),
        cost_estimate=pl.CostEstimate(flops=2 * macs, bytes_accessed=8 * FQ * B * 4, transcendentals=FQ * B),
        name="cg",
    )(gate_pre, up_pre, token_weight[None, :], query_grad)


def solution(mesh):
    placed = (P("seq", "tp"), P("seq", "tp"), P("seq"), P("tp", "seq"))
    return jax.shard_map(
        local,
        mesh=mesh,
        in_specs=placed,
        out_specs=(P("tp", "seq"), P("tp", "seq")),
        check_vma=False,
    )
```

```python
import jax
import jax.numpy as jnp
from jax import lax
from jax.experimental import pallas as pl
from jax.experimental.pallas import tpu as pltpu
from jax.sharding import PartitionSpec as P

DAMP = 1.0
F32, BF16 = jnp.float32, jnp.bfloat16
MESH = pl.DeviceIdType.MESH

B = 128
FQ = 1792
R = 32
UNITS = [(0, 0), (1, 0), (3, 0), (0, 1), (0, 3), (2, 0), (0, 2), (3, 3), (1, 1), (3, 1), (1, 3), (2, 1), (2, 3), (1, 2), (3, 2), (2, 2)]
SLOT = {u: i for i, u in enumerate(UNITS)}
UT = 2 * B
T = len(UNITS) * UT
GROUPS0 = [(0, 1), (1, 3), (3, 5), (5, 7), (7, 9), (9, 11), (11, 13), (13, 15), (15, 16)]
GROUPS1 = [(0, 1), (1, 3), (3, 5), (5, 7), (7, 9), (9, 11), (11, 13), (13, 15), (15, 16)]
RELAYED = 6
SEMS = {"send": 18, "recv": 70}


def kernel(gate, up, tw, q, x_out, r_out, H, nblk, hl_s, hl, qv, qb, z0, zb, z1, yown, yst, rs, ymid, yfar, sT, wb, wrow, acc, sc, dv, rn, d_r, r_s, r_r, ssem, rsem):
    s, t = lax.axis_index("seq"), lax.axis_index("tp")
    y, xh, z = s // 8, (s // 4) % 2, s % 4
    xl, k = t // 2, t % 2
    x = xh * 2 + xl

    def dev(x, y, z, k):
        return (y * 8 + (x // 2) * 4 + z, (x % 2) * 2 + k)

    def ystep(d):
        return dev(x, (y + d) % 4, z, k)

    def zstep(d):
        return dev(x, y, (z + d) % 4, k)

    def xstep(d):
        return dev((x + d) % 4, y, z, k)

    sib = dev(x, y, z, 1 - k)
    partner = dev((x + 2) % 4, y, z, 1 - k)
    moved = k != xh

    barrier = pltpu.get_barrier_semaphore()
    peers = [dev((x + d) % 4, y, z, c) for d in range(4) for c in (k, 1 - k)][1:]
    plane = [(dy, dz) for dy in range(4) for dz in range(4)][1:]
    peers += [dev(x, (y + dy) % 4, (z + dz) % 4, k) for dy, dz in plane]
    for p in peers:
        pl.semaphore_signal(barrier, inc=1, device_id=p, device_id_type=MESH)

    used = {"send": 0, "recv": 0}

    def take(kind):
        used[kind] += 1
        assert used[kind] <= SEMS[kind]
        return used[kind] - 1

    class Copies:
        def __init__(self, sends, recv=None):
            self.sends, self.recv = sends, take("recv") if recv is None else recv

        def make(self, src, dst, device):
            return pltpu.make_async_remote_copy(src_ref=src, dst_ref=dst, send_sem=ssem.at[self.sends], recv_sem=rsem.at[self.recv], device_id=device, device_id_type=MESH)

        def push(self, src, dst, device):
            self.make(src, dst, device).start()

        def wait(self, whole):
            pltpu.make_async_copy(whole, whole, rsem.at[self.recv]).wait()

    def drain(sends, whole):
        pltpu.make_async_copy(whole, whole, ssem.at[sends]).wait()

    wb[0, 0] = jnp.broadcast_to(tw[...].astype(F32) * (1.0 / T), (8, B))

    def block(yr, zr, core=0, off=0, n=B):
        return H.at[pl.ds(SLOT[yr, zr] * UT + core * B + off, n)]

    hops = take("send")

    def hop(yr, zr, axis, d, off, n, copies):
        if axis == "y":
            return copies.make(block(yr, zr, 0, off, n), block((yr - d) % 4, zr, 0, off, n), ystep(d))
        return copies.make(block(yr, zr, 0, off, n), block(yr, (zr - d) % 4, 0, off, n), zstep(d))

    h_sends = take("send")
    h_moves = [Copies(h_sends) for _ in range(4)]
    sides = [("y", 1), ("z", 1), ("y", -1), ("z", -1)]
    s1 = {(a, 1, h): Copies(hops) for a in "yz" for h in range(2)}
    s1.update({(a, -1): Copies(hops) for a in "yz"})
    w_copies = Copies(take("send"))

    def own_piece(i):
        for a, d in sides:
            hop(0, 0, a, d, i * 32, 32, s1[(a, 1, i // 2) if d == 1 else (a, -1)]).start()

    for i in range(4):

        @pl.loop(0, 2)
        def _(h):
            rows = pl.ds(pl.multiple_of(i * 32 + h * 16, 16), 16)
            g, u = gate[rows, :].astype(F32), up[rows, :].astype(F32)
            nblk[rows, :] = (g / (1.0 + jnp.exp(-g)) * u).astype(BF16)

        if i == 0:
            pl.semaphore_wait(barrier, len(peers))

        @pl.when(moved)
        def _():
            h_moves[i].push(nblk.at[pl.ds(i * 32, 32)], block(0, 0, 0, i * 32, 32), partner)

        @pl.when(jnp.logical_not(moved))
        def _():
            block(0, 0, 0, i * 32, 32)[...] = nblk[i * 32 : (i + 1) * 32]
            own_piece(i)

    for dy, dz in plane:
        w_copies.push(wb.at[0, 0], wb.at[0, (4 - dz) % 4 * 4 + (4 - dy) % 4], dev(x, (y + dy) % 4, (z + dz) % 4, k))

    @pl.when(moved)
    def _():
        for i in range(4):
            h_moves[i].wait(block(0, 0, 0, 0, 32))
            own_piece(i)

    relay_sends = take("send")
    relay_groups = [Copies(relay_sends) for _ in GROUPS0]

    def relay(yr, zr):
        g = [SLOT[yr, zr] < e for _, e in GROUPS0].index(True)
        relay_groups[g].push(block(yr, zr, 0), block(yr, zr, 1), sib)

    relay(0, 0)

    for i in range(FQ // B):
        cols = slice(i * B, (i + 1) * B)
        hl_s[:, cols] = q[cols, :].T.astype(BF16)
    q_move = Copies(take("send"))

    @pl.when(moved)
    def _():
        for i in range(4):
            q_move.push(hl_s.at[pl.ds(i * 32, 32)], hl.at[pl.ds(i * 32, 32)], partner)

    def rows_of(n):
        return H.at[pl.ds(0, n)]

    s2 = Copies(hops)
    s1["y", 1, 0].wait(rows_of(64))
    hop(3, 0, "y", 1, 0, 64, s2).start()
    s1["z", 1, 0].wait(rows_of(64))
    hop(0, 3, "z", 1, 0, 64, s2).start()
    s1["y", -1].wait(rows_of(128))
    relay(1, 0)
    hop(1, 0, "y", -1, 64, 64, s2).start()
    s1["z", -1].wait(rows_of(128))
    relay(0, 1)
    hop(0, 1, "z", -1, 64, 64, s2).start()
    s1["y", 1, 1].wait(rows_of(64))
    relay(3, 0)
    s1["z", 1, 1].wait(rows_of(64))
    relay(0, 3)
    corners = [(3, 0, "z", 1), (1, 0, "z", -1), (0, 1, "y", 1), (0, 3, "y", -1)]
    s3 = [Copies(hops), Copies(hops)]
    for c in corners:
        hop(*c, 64, 64, s3[0]).start()
    for c in corners:
        hop(*c, 0, 64, s3[1]).start()
    w_copies.wait(wb.at[0, pl.ds(1, 15)])
    w_swap = Copies(take("send"))
    w_swap.push(wb.at[0], wb.at[1], partner)

    @pl.when(moved)
    def _():
        q_move.wait(hl)

    @pl.when(jnp.logical_not(moved))
    def _():
        hl[...] = hl_s[...]

    bases = [pl.multiple_of(((x + j) % 4) * R, R) for j in range(4)]
    for j in range(4):
        qb[j * R : (j + 1) * R, :] = hl[pl.ds(bases[j], R), :]
    z0[...] = jnp.zeros_like(z0)
    z1[...] = jnp.zeros_like(z1)
    acc[...] = jnp.zeros_like(acc)

    rs_copies, ag_copies = [], []
    rs_sends, ag_sends = [take("send"), take("send")], [take("send"), take("send")]
    for it, groups in enumerate((GROUPS0, GROUPS1)):
        before = list(zip(rs_copies[0].values(), ag_copies[0].values())) if it else [(None, None)] * len(groups)
        rs_copies.append({g: Copies(rs_sends[it], a and a.recv) for g, (a, _) in zip(groups, before)})
        ag_copies.append({g: Copies(ag_sends[it], a and a.recv) for g, (_, a) in zip(groups, before)})

    onward = [{}, {g: Copies(ag_sends[1]) for g in GROUPS1[:RELAYED]}]
    far_part = {g: Copies(rs_sends[1]) for g in GROUPS1[:RELAYED]}

    def cols_of(group):
        return group[0] * UT, (group[1] - group[0]) * UT

    def image(it, p, group):
        c, n = cols_of(group)
        at = pl.ds(c, n)
        part = lax.dot_general(p[...], H[at, :], (((1,), (1,)), ((), ())), preferred_element_type=F32)
        yown[it, :, at] = part[:R]
        if group in onward[it]:
            ymid[0, :, at] = part[R : 2 * R]
            ymid[1, :, at] = part[3 * R :]
            yst[it, pl.ds(R, R), at] = part[2 * R : 3 * R].astype(BF16)
            far_part[group].push(yst.at[it, pl.ds(R, R // 2), at], yfar.at[0, :, at], xstep(1))
            far_part[group].push(yst.at[it, pl.ds(R + R // 2, R // 2), at], yfar.at[1, :, at], xstep(3))
            return
        yst[it, :, at] = part[R:].astype(BF16)
        for j in (2, 1, 3):
            rs_copies[it][group].push(yst.at[it, pl.ds((j - 1) * R, R), at], rs.at[it, 3 - j, :, at], xstep(j))

    def middle(it, group):
        at = pl.ds(*cols_of(group))
        far_part[group].wait(yfar.at[:, :, at])
        top, low = pl.ds(0, R // 2), pl.ds(R // 2, R // 2)
        yst[it, top, at] = (ymid[0, top, at] + yfar[0, :, at].astype(F32)).astype(BF16)
        yst[it, low, at] = ymid[0, low, at].astype(BF16)
        yst[it, pl.ds(2 * R, R // 2), at] = ymid[1, top, at].astype(BF16)
        yst[it, pl.ds(2 * R + R // 2, R // 2), at] = (ymid[1, low, at] + yfar[1, :, at].astype(F32)).astype(BF16)
        for j in (1, 3):
            rs_copies[it][group].push(yst.at[it, pl.ds((j - 1) * R, R), at], rs.at[it, 3 - j, :, at], xstep(j))

    def reduce(it, group, between=None):
        every = pl.ds(*cols_of(group))
        near_only = group in onward[it]
        rs_copies[it][group].wait(rs.at[it, pl.ds(0, 2 if near_only else 3), :, every])

        @pl.loop(group[0], group[1])
        def _(u):
            at = pl.ds(pl.multiple_of(u * UT, UT), UT)
            total = yown[it, :, at] + rs[it, 0, :, at].astype(F32) + rs[it, 2, :, at].astype(F32)
            if not near_only:
                total = total + rs[it, 1, :, at].astype(F32)
            scaled = (total * wrow[0:1, at]).astype(BF16)
            sT[it, pl.ds(0, R), at] = scaled
            if it:
                acc[...] += total * scaled.astype(F32)

        if between:
            between()
        for j in (1, 3) if group in onward[it] else (2, 1, 3):
            ag_copies[it][group].push(sT.at[it, pl.ds(0, R), every], sT.at[it, pl.ds((4 - j) * R, R), every], xstep(j))

    def forward(it, group):
        at = pl.ds(*cols_of(group))
        ag_copies[it][group].wait(sT.at[it, pl.ds(R, 2 * R), at])
        onward[it][group].push(sT.at[it, pl.ds(3 * R, R // 2), at], sT.at[it, pl.ds(2 * R, R // 2), at], xstep(1))
        onward[it][group].push(sT.at[it, pl.ds(R + R // 2, R // 2), at], sT.at[it, pl.ds(2 * R + R // 2, R // 2), at], xstep(3))

    def back(it, zz, group):
        at = pl.ds(*cols_of(group))
        if group in onward[it]:
            onward[it][group].wait(sT.at[it, pl.ds(2 * R, R), at])
        else:
            ag_copies[it][group].wait(sT.at[it, pl.ds(R, 3 * R), at])
        zz[...] += jnp.dot(sT[it, :, at], H[at, :], preferred_element_type=F32)

    G = GROUPS0

    def img(i):
        lo, hi = G[i]
        relay_groups[i].wait(rows_of((hi - lo) * B))
        image(0, qb, G[i])

    def red(i):
        reduce(0, G[i])

    def bck(i):
        back(0, z0, G[i])

    img(0)
    img(1)
    s2.wait(rows_of(256))
    relay(2, 0)
    relay(0, 2)
    img(2)
    w_swap.wait(wb.at[1])
    other = jnp.where(moved, 1, 0)
    for u, (yr, zr) in enumerate(UNITS):
        for c in range(2):
            wrow[0:8, u * UT + c * B : u * UT + (c + 1) * B] = wb[(other + c) % 2, zr * 4 + yr]
    s3[0].wait(rows_of(256))
    s4, s5, s6 = Copies(hops), Copies(hops), Copies(hops)
    for c in ((2, 0, "z", 1, 0, 64), (2, 0, "z", -1, 0, 64), (3, 1, "y", 1, 64, 32), (1, 1, "y", -1, 96, 32), (3, 3, "y", 1, 64, 32), (1, 3, "y", -1, 96, 32)):
        hop(*c, s4).start()
    red(0)
    img(3)
    red(1)
    s3[1].wait(rows_of(256))
    for u in UNITS[7:11]:
        relay(*u)
    for c in ((0, 2, "y", 1, 0, 64), (0, 2, "y", -1, 0, 64), (1, 3, "z", 1, 64, 32), (1, 1, "z", -1, 96, 32), (3, 3, "z", 1, 64, 32), (3, 1, "z", -1, 96, 32)):
        hop(*c, s5).start()
    red(2)
    for j in range(4):
        qv[j * R : (j + 1) * R, :] = qb[j * R : (j + 1) * R, :].astype(F32)
    red(3)
    img(4)
    bck(0)
    img(5)
    bck(1)
    s4.wait(rows_of(256))
    hop(2, 3, "z", 1, 0, 32, s6).start()
    hop(2, 1, "z", -1, 32, 32, s6).start()
    relay(2, 1)
    relay(2, 3)
    bck(2)
    red(4)
    img(6)
    red(5)
    s5.wait(rows_of(256))
    hop(3, 2, "y", 1, 64, 32, s6).start()
    hop(1, 2, "y", -1, 96, 32, s6).start()
    relay(1, 2)
    relay(3, 2)
    bck(3)
    bck(4)
    red(6)
    img(7)
    s6.wait(rows_of(128))
    relay(2, 2)
    bck(5)
    img(8)
    red(7)
    bck(6)
    red(8)
    bck(7)
    bck(8)

    zb[...] = z0[...].astype(BF16)

    def total_of(v):
        return jnp.sum(jnp.sum(v, axis=0, keepdims=True), axis=1, keepdims=True)

    sums = {}

    def spread(which, phase):
        src, copies = sc.at[which, phase, 0], Copies(take("send"))
        sums[which, phase] = copies
        if phase == 0:
            to = [(1, 1 - k), (2, k), (2, 1 - k), (3, 1 - k), (1, k), (3, k), (0, 1 - k)]
            for (d, c), i in zip(to, [3, 2, 6, 1, 7, 5, 4]):
                copies.push(src, sc.at[which, 0, i], dev((x + d) % 4, y, z, c))
        else:
            for dy, dz in plane:
                copies.push(src, sc.at[which, 1, (4 - dy) % 4 * 4 + (4 - dz) % 4], dev(x, (y + dy) % 4, (z + dz) % 4, k))

    def collect(which, phase):
        sums[which, phase].wait(sc.at[which, phase, pl.ds(1, 7 if phase == 0 else 15)])
        got = sc[which, phase, 0]
        for i in range(1, 8 if phase == 0 else 16):
            got = got + sc[which, phase, i]
        sc[which, phase + 1, 0] = got

    G = GROUPS1
    N = len(G)
    z_move = Copies(take("send"))

    def swap_rows(lo, hi):
        @pl.when(moved)
        def _():
            for j in range(lo, hi):
                z_move.push(zb.at[pl.ds(j * R, R)], d_r.at[pl.ds(bases[j], R)], partner)

    swap_rows(0, 1)
    image(1, zb, G[0])
    image(1, zb, G[1])
    swap_rows(1, 4)

    def moments(i, m):
        rows = pl.ds(pl.multiple_of(i * 8, 8), 8)
        qr, zr = qv[rows, :], z0[rows, :]
        return m[0] + qr * qr, m[1] + qr * zr, m[2] + zr * zr

    zero = jnp.zeros((8, FQ), F32)
    mm = lax.fori_loop(0, B // 8, moments, (zero, zero, zero))
    row = lax.broadcasted_iota(jnp.int32, (8, B), 0)
    sc[0, 0, 0] = jnp.where(row == 0, total_of(mm[0]), jnp.where(row == 1, total_of(mm[1]), total_of(mm[2])))
    spread(0, 0)
    image(1, zb, G[2])
    middle(1, G[0])
    image(1, zb, G[3])
    middle(1, G[1])

    def ring_sum():
        sc[1, 0, 0] = jnp.broadcast_to(total_of(acc[...]), (8, B))
        spread(1, 0)

    for i in range(N):
        if i + 2 < RELAYED:
            middle(1, G[i + 2])
        if i + 4 < N:
            image(1, zb, G[i + 4])
        reduce(1, G[i], ring_sum if i == N - 1 else None)
        if 2 <= i < RELAYED + 2:
            forward(1, G[i - 2])
        if i >= 4:
            back(1, z1, G[i - 4])
        if i == 3:
            collect(0, 0)
            spread(0, 1)
        if i == 6:
            collect(0, 1)
            m = sc[0, 2, 0]
            m0, m1, m2 = m[0:1, 0:1], m[1:2, 0:1], m[2:3, 0:1]
            al0 = m0 / (m1 + DAMP * m0)
            n1 = al0 * al0 * (m2 - m1 * m1 / m0)
            beta = n1 / m0
            for j in range(4):
                base = bases[j]

                @pl.loop(0, R // 16)
                def _(h):
                    rows = pl.ds(pl.multiple_of(j * R + h * 16, 16), 16)
                    to = pl.ds(pl.multiple_of(base + h * 16, 16), 16)
                    qr = qv[rows, :]
                    d1 = qr - al0 * (z0[rows, :] + DAMP * qr) + beta * qr
                    dv[to, :] = d1

    for i in range(N - 4, N - 1):
        back(1, z1, G[i])

    @pl.when(jnp.logical_not(moved))
    def _():
        for i in range(FQ // B):
            cols = slice(i * B, (i + 1) * B)
            x_out[cols, :] = dv[:, cols].T

    @pl.when(moved)
    def _():
        z_move.wait(d_r)
        for i in range(FQ // B):
            cols = slice(i * B, (i + 1) * B)
            x_out[cols, :] = (1.0 - DAMP * al0 + beta) * q[cols, :] - al0 * d_r[:, cols].astype(F32).T

    collect(1, 0)
    spread(1, 1)
    back(1, z1, G[N - 1])

    cz = 1.0 - DAMP * al0 + beta

    @pl.loop(0, B // 16)
    def _(i):
        rows = pl.ds(pl.multiple_of(i * 16, 16), 16)
        qr, z0r = qv[rows, :], z0[rows, :]
        r1 = qr - al0 * (z0r + DAMP * qr)
        z0[rows, :] = r1
        z1[rows, :] = cz * z0r - al0 * z1[rows, :] + DAMP * (r1 + beta * qr)

    m = sc[0, 1, 0]
    o0, o1, o2 = m[0:1, 0:1], m[1:2, 0:1], m[2:3, 0:1]
    o3 = sc[1, 1, 0][0:1, 0:1]
    keep = 1.0 - DAMP * al0
    top = keep * keep * o0 - 2.0 * al0 * keep * o1 + al0 * al0 * o2
    low = DAMP * (top + 2.0 * beta * (keep * o0 - al0 * o1) + beta * beta * o0) + cz * cz * o1 - 2.0 * cz * al0 * o2 + al0 * al0 * o3
    near = jnp.where((top > 0.0) & (low > 0.0), top / low, 1.0)
    near = jnp.where((near > 1e-6) & (near < 1e6), near, 1.0)
    W = 2 * B
    r_sends = take("send")
    r_moves = [Copies(r_sends) for _ in range(FQ // W)]

    @pl.when(moved)
    def _():
        for i in range(FQ // W):
            cols = slice(i * W, (i + 1) * W)
            for j in range(4):
                rows = slice(j * R, (j + 1) * R)
                r_s[pl.ds(bases[j], R), cols] = (z0[rows, cols] - near * z1[rows, cols]).astype(BF16)
            part = pl.ds(i * W, W)
            r_moves[i].push(r_s.at[:, part], r_r.at[:, part], partner)

    drain(hops, rows_of(1920))
    drain(relay_sends, rows_of(16 * B))
    for it in range(2):
        drain(rs_sends[it], yst.at[it])
        drain(ag_sends[it], sT.at[it, pl.ds(R, 3 * R)])
    drain(w_copies.sends, wb.at[0, pl.ds(1, 15)])
    drain(w_swap.sends, wb.at[1])
    for which, phase in sums:
        drain(sums[which, phase].sends, sc.at[which, phase, pl.ds(1, 7 if phase == 0 else 15)])

    @pl.when(jnp.logical_not(moved))
    def _():
        for i in range(FQ // B):
            cols = slice(i * B, (i + 1) * B)
            for j in range(4):
                rows = slice(j * R, (j + 1) * R)
                rn[pl.ds(bases[j], R), cols] = z0[rows, cols] - near * z1[rows, cols]
            r_out[cols, :] = rn[:, cols].T

    collect(1, 1)
    m3 = sc[1, 2, 0][0:1, 0:1]
    al1 = n1 / (DAMP * (n1 + beta * beta * m0) + cz * cz * m1 - 2.0 * cz * al0 * m2 + al0 * al0 * m3)
    ratio = al1 / near

    @pl.when(jnp.logical_not(moved))
    def _():
        @pl.loop(0, FQ // B)
        def _(i):
            rows = pl.ds(pl.multiple_of(i * B, B), B)
            qr, d1 = q[rows, :], x_out[rows, :]
            r_out[rows, :] = ratio * r_out[rows, :] + (1.0 - ratio) * (d1 - beta * qr)
            x_out[rows, :] = al0 * qr + al1 * d1

    @pl.when(moved)
    def _():
        @pl.loop(0, FQ // B)
        def _(i):
            rows = pl.ds(pl.multiple_of(i * B, B), B)
            qr, d1 = q[rows, :], x_out[rows, :]
            r_out[rows, :] = (1.0 - ratio) * (d1 - beta * qr)
            x_out[rows, :] = al0 * qr + al1 * d1

        for i in range(FQ // W):
            r_moves[i].wait(r_r.at[:, pl.ds(i * W, W)])
            for c in range(i * 2, i * 2 + 2):
                cols = slice(c * B, (c + 1) * B)
                r_out[cols, :] += ratio * r_r[:, cols].astype(F32).T
        drain(h_sends, nblk)
        drain(q_move.sends, hl_s)
        drain(z_move.sends, zb)
        drain(r_sends, r_s)


def local(gate_pre, up_pre, token_weight, query_grad):
    vmem = pl.BlockSpec(memory_space=pltpu.VMEM)
    out = jax.ShapeDtypeStruct((FQ, B), F32)
    macs = 4 * T * FQ * B
    return pl.pallas_call(
        kernel,
        out_shape=(out, out),
        in_specs=[vmem] * 4,
        out_specs=(vmem, vmem),
        scratch_shapes=[
            pltpu.VMEM((T, FQ), BF16),
            pltpu.VMEM((B, FQ), BF16),
            pltpu.VMEM((B, FQ), BF16),
            pltpu.VMEM((B, FQ), BF16),
            pltpu.VMEM((B, FQ), F32),
            pltpu.VMEM((B, FQ), BF16),
            pltpu.VMEM((B, FQ), F32),
            pltpu.VMEM((B, FQ), BF16),
            pltpu.VMEM((B, FQ), F32),
            pltpu.VMEM((2, R, T), F32),
            pltpu.VMEM((2, 3 * R, T), BF16),
            pltpu.VMEM((2, 3, R, T), BF16),
            pltpu.VMEM((2, R, T), F32),
            pltpu.VMEM((2, R // 2, T), BF16),
            pltpu.VMEM((2, B, T), BF16),
            pltpu.VMEM((2, 16, 8, B), F32),
            pltpu.VMEM((8, T), F32),
            pltpu.VMEM((R, UT), F32),
            pltpu.VMEM((2, 3, 16, 8, B), F32),
            pltpu.VMEM((B, FQ), F32),
            pltpu.VMEM((B, FQ), F32),
            pltpu.VMEM((B, FQ), BF16),
            pltpu.VMEM((B, FQ), BF16),
            pltpu.VMEM((B, FQ), BF16),
            pltpu.SemaphoreType.DMA((SEMS["send"],)),
            pltpu.SemaphoreType.DMA((SEMS["recv"],)),
        ],
        compiler_params=pltpu.CompilerParams(collective_id=0, has_side_effects=True, vmem_limit_bytes=56 * 2**20),
        cost_estimate=pl.CostEstimate(flops=2 * macs, bytes_accessed=8 * FQ * B * 4, transcendentals=FQ * B),
        name="cg",
    )(gate_pre, up_pre, token_weight[None, :], query_grad)


def solution(mesh):
    placed = (P("seq", "tp"), P("seq", "tp"), P("seq"), P("tp", "seq"))
    return jax.shard_map(
        local,
        mesh=mesh,
        in_specs=placed,
        out_specs=(P("tp", "seq"), P("tp", "seq")),
        check_vma=False,
    )
```
